768 devices in a mesh: grp: 32 (over z_lo, y), shard: 24 (over z_hi, x, core).
Axes of the slice: x: 4, y: 8, z: 12 (z_hi: 3, z_lo: 4; z = z_hi * 4 + z_lo), core: 2. Of those that a mesh axis runs over, the one named last changes fastest.
Arguments:
- features: bfloat16 [196608, 1536], P(('grp', 'shard')), may hold values from -6 to 6
- w_in: bfloat16 [1536, 1024], replicated, may hold values from -0.15625 to 0.15625
- upstream: bfloat16 [196608, 1024], P(('grp', 'shard')), may hold values from -6 to 6
- hot_ids: int32 [196608, 8], P(('grp', 'shard')), may hold values from 0 to 6143
- cold_rows: int32 [786432], P(('grp', 'shard')), may hold values from 0 to 2047
- cold_owner: int32 [786432, 1], P(('grp', 'shard')), may hold values from 0 to 23; in each aligned block of 1024 rows (0 to 1023, 1024 to 2047, ...) at most 170 rows name the same one
- hot_table: float32 [6144, 128], P('shard'), may hold values from -6 to 6
- hot_accum: float32 [6144], P('shard'), may hold values from 1 to 1000
- cold_table: float32 [1572864, 128], P(('grp', 'shard')), may hold values from -6 to 6
- cold_accum: float32 [1572864], P(('grp', 'shard')), may hold values from 1 to 1000
Outputs:
- hot_new: float32 [6144, 128], P('shard')
- hot_accum_new: float32 [6144], P('shard')
- cold_new: float32 [1572864, 128], P(('grp', 'shard'))
- cold_accum_new: float32 [1572864], P(('grp', 'shard'))
The draws below stay inside these ranges and needn't reach their ends.
Inputs may be any that keep to these rules, and one draw needn't show every extreme that they name: `cold_owner`: among the 1024 lookups of one device, no owner is named more than 170 times, a bound that some block reaches.
All inputs are finite; a program needn't handle non-finite values.
Results may differ from the reference program's by a relative error of at most 0.0024.
Values may be sent and summed in bfloat16 or wider, within the bound.
A program may use at most 64 MiB of HBM per device.

```python
import math
import jax
import jax.numpy as jnp
import numpy as np
from jax import lax

E = 128
H = 1024
FH = 8
FC = 4
TOK_DEV = 256
COLD_DEV = 2048
FE = 1536
HOT = 6144
COLD = 1572864
TOKENS = 196608
LC = 1024
CAP = 170
N_GRP = 32
N_SHARD = 24


def set_ends(drawn, key, smallest, top_value):
    longest = drawn.shape.index(max(drawn.shape))
    spots = []
    for shift in (0, 1):
        where = [jax.random.randint(jax.random.fold_in(key, axis), (), 0, length) for axis, length in enumerate(drawn.shape)]
        where[longest] = (where[longest] + shift) % drawn.shape[longest]
        spots.append(tuple(where))
    return drawn.at[spots[0]].set(smallest).at[spots[1]].set(top_value)


def shard_levels(key, dims, cuts, low, top_value):
    loudness = 1.0
    for axis_at, parts in cuts:
        draws = jax.random.uniform(jax.random.fold_in(jax.random.fold_in(key, 6), axis_at), (parts,), jnp.float32, low / len(cuts), top_value / len(cuts))
        loudness = loudness * jnp.repeat(jnp.exp(draws), dims[axis_at] // parts).reshape((-1,) + (1,) * (len(dims) - 1 - axis_at))
    return loudness


def rank_table(amount, lean):
    portions = [(1 << 20) // math.isqrt(grade ** lean) + 1 for grade in range(1, amount + 1)]
    width = 1 + sum(portions) // (1 << 30)
    return np.cumsum(np.array([max(1, weight // width) for weight in portions]))


def ranked_ids(key, shape, number_of, lean):
    grid = rank_table(number_of, lean)
    pick = jax.random.randint(jax.random.fold_in(key, 1), shape, 0, int(grid[number_of - 1]))
    grade = jnp.searchsorted(jnp.asarray(grid, jnp.int32), pick, side="right")
    return jax.random.permutation(jax.random.fold_in(key, 2), number_of)[grade].astype(jnp.int32)


def routed_block(key, own, number, rows, number_of, top, limit, lean):
    ranking = jax.random.permutation(key, number_of)
    crowded, ordinary = portions_of(number_of, rows * top, limit, lean, True), portions_of(number_of, rows * top, limit, lean, False)
    places = jnp.arange(number_of)

    def named(lengths, turn):
        used = int((lengths > 0).sum())
        fixed = max(1, used // 4)
        moved = fixed + (places - fixed + turn * (used - fixed)) % max(1, number_of - fixed)
        return jnp.zeros((number_of,), jnp.int32).at[ranking[jnp.where(places < fixed, places, moved)]].set(jnp.asarray(lengths, jnp.int32))

    lengths = jnp.where(number % 4 == 0, named(crowded, number // 4), named(ordinary, number - number // 4 - 1))
    mixed = jax.random.permutation(jax.random.fold_in(own, 3), number_of)
    donor, receiver = mixed[0:number_of // 2 * 2:2], mixed[1:number_of // 2 * 2:2]
    margin = jnp.minimum(lengths[donor] - 1, limit - lengths[receiver]) // 2
    margin = jnp.where((donor == ranking[0]) | (receiver == ranking[0]) | (lengths[receiver] == 0), 0, jnp.maximum(margin, 0))
    moved = jax.random.randint(jax.random.fold_in(own, 4), (number_of // 2,), 0, 1 << 20) % (margin + 1)
    lengths = lengths.at[donor].add(-moved).at[receiver].add(moved)
    items = jnp.searchsorted(jnp.cumsum(lengths), jnp.arange(rows * top), side="right").astype(jnp.int32)
    grid = items.reshape(top, rows).T
    grid = grid[jax.random.permutation(jax.random.fold_in(own, 1), rows)]
    turn = jax.random.randint(jax.random.fold_in(own, 2), (rows, 1), 0, top)
    return jnp.take_along_axis(grid, (jnp.arange(top)[None, :] + turn) % top, axis=1)


def portions_of(count, total, reach, lean, full):
    weights = [(1 << 20) // math.isqrt(standing ** lean) + 1 for standing in range(1, count + 1)]
    largest = reach if full else min(reach, max(-(-total // count), total * weights[0] // sum(weights)))
    least = 1 if total - largest >= count - 1 else 0
    counts, surplus = [largest] + [least] * (count - 1), total - largest - least * (count - 1)
    while surplus > 0:
        movable = [i for i in range(1, count) if counts[i] < largest] or [i for i in range(1, count) if counts[i] < reach]
        pool, left = sum([weights[i] for i in movable]), surplus
        for i in movable:
            more = min(reach - counts[i], max(1, left * weights[i] // pool), surplus)
            counts[i] = counts[i] + more
            surplus = surplus - more
    return np.array(counts)


def bell_draw(own_key, extent, width, limit, shards=(), kind=jnp.bfloat16):
    drawn = jax.random.normal(own_key, extent, jnp.float32) * width
    if len(shards) > 0:
        drawn = shard_levels(own_key, extent, shards, -0.22, 0.18) * drawn
    return jnp.clip(drawn, min=-limit, max=limit).astype(kind)


def setup_inputs(seed: int = 0) -> dict:
    seeds = jax.random.split(jax.random.key(seed), 11)
    features = bell_draw(seeds[0], (TOKENS, FE), 1.0, 6.0, ((0, 768),))
    w_in = bell_draw(seeds[1], (FE, H), FE ** -0.5, 0.15625)
    upstream = bell_draw(seeds[2], (TOKENS, H), 1.0, 6.0, ((0, 768),))
    hot_ids = set_ends(ranked_ids(seeds[3], (TOKENS, FH), HOT, 1), jax.random.fold_in(seeds[3], 3), 0, HOT - 1).astype(jnp.int32)
    cold_rows = set_ends(ranked_ids(seeds[4], (TOKENS * FC,), COLD_DEV, 1), jax.random.fold_in(seeds[4], 3), 0, COLD_DEV - 1).astype(jnp.int32)
    cold_owner_keys = jax.random.split(jax.random.fold_in(seeds[5], 1), (TOKENS * FC) // LC)
    cold_owner_turns = jax.random.permutation(jax.random.fold_in(seeds[5], 3), (TOKENS * FC) // LC)
    cold_owner = jax.vmap(lambda own, number: routed_block(jax.random.fold_in(seeds[5], 2), own, number, LC, N_SHARD, 1, CAP, 2))(cold_owner_keys, cold_owner_turns).reshape((TOKENS * FC, 1))
    hot_table = bell_draw(seeds[6], (HOT, E), 1.0, 6.0, ((0, 24),), jnp.float32)
    hot_accum = jnp.clip(jnp.exp(math.log(1000.0) - 6.9077553 * jax.random.uniform(seeds[7], (HOT,), jnp.float32) ** shard_levels(seeds[7], (HOT,), ((0, 24),), -0.2, 0.2)), 1.0, 1000.0)
    cold_table = bell_draw(seeds[8], (COLD, E), 1.0, 6.0, ((0, 768),), jnp.float32)
    cold_accum = jnp.clip(jnp.exp(math.log(1000.0) - 6.9077553 * jax.random.uniform(seeds[9], (COLD,), jnp.float32) ** shard_levels(seeds[9], (COLD,), ((0, 768),), -0.2, 0.2)), 1.0, 1000.0)
    return dict(features=features, w_in=w_in, upstream=upstream, hot_ids=hot_ids, cold_rows=cold_rows, cold_owner=cold_owner, hot_table=hot_table, hot_accum=hot_accum, cold_table=cold_table, cold_accum=cold_accum)


learn_rate = 0.5

def backward_rows(features, w_in, upstream):
    preact = jnp.dot(features, w_in, preferred_element_type=jnp.float32)
    sigm = jax.nn.sigmoid(preact)
    delta = (upstream.astype(jnp.float32) * sigm * (1.0 + preact * (1.0 - sigm))).astype(jnp.bfloat16)
    return jnp.dot(delta, w_in.T, preferred_element_type=jnp.float32).astype(jnp.bfloat16)

def adagrad(rows, accum, grads):
    accum_new = accum + lax.optimization_barrier(jnp.mean(grads * grads, axis=1))
    return (rows - learn_rate * grads / jnp.sqrt(accum_new)[:, None], accum_new)

def reference(features, w_in, upstream, hot_ids, cold_rows, cold_owner, hot_table, hot_accum, cold_table, cold_accum):
    blocks = features.reshape(N_GRP * 8, -1, FE)
    up_blocks = upstream.reshape(N_GRP * 8, -1, H)
    grads_in = lax.map(lambda pair: backward_rows(pair[0], w_in, pair[1]), (blocks, up_blocks)).reshape(TOKENS, FE)
    hot_rows_all = grads_in[:, :FH * E].reshape(N_GRP * N_SHARD, TOK_DEV * FH, E)
    hot_ids_all = hot_ids.reshape(N_GRP * N_SHARD, TOK_DEV * FH)

    def add_device(total, pair):
        term = jax.ops.segment_sum(pair[0].astype(jnp.float32), pair[1], num_segments=HOT)
        return (total + term, None)
    hot_sum, unused = lax.scan(add_device, jnp.zeros((HOT, E), jnp.float32), (hot_rows_all, hot_ids_all))
    cold_part = grads_in[:, FH * E:].reshape(TOKENS * FC, E).astype(jnp.float32)
    source = jnp.arange(TOKENS * FC, dtype=jnp.int32) // (TOK_DEV * FC)
    owner_dev = source // N_SHARD * N_SHARD + cold_owner[:, 0]
    cold_sum = jax.ops.segment_sum(cold_part, owner_dev * COLD_DEV + cold_rows, num_segments=COLD)
    hot_new, hot_accum_new = adagrad(hot_table, hot_accum, hot_sum)
    cold_new, cold_accum_new = adagrad(cold_table, cold_accum, cold_sum)
    return (hot_new, hot_accum_new, cold_new, cold_accum_new)
```

```python
import jax
import jax.numpy as jnp
from jax import lax
from jax.experimental import pallas as pl
from jax.experimental.pallas import tpu as pltpu
from jax.sharding import PartitionSpec as P

MESH = pl.DeviceIdType.MESH
learn_rate = 0.5

E = 128
SAMPLES = 256
HOT_FIELDS, COLD_FIELDS = 8, 4
OWNERS = 24
SLOTS = 176
USED = 170
HEAD = 168
DEPTH = 256
OWNED = 2048
STEP = 256
BF16, F32, I32 = jnp.bfloat16, jnp.float32, jnp.int32


def iota(shape, axis):
    return lax.broadcasted_iota(I32, shape, axis)


def nt_dot(a, b):
    return lax.dot_general(a, b, (((1,), (1,)), ((), ())), preferred_element_type=F32)


def dot(a, b):
    return jnp.dot(a, b, preferred_element_type=F32)


def grads_kernel(
    feat_ref, w_ref, up_ref, hid_ref, row_ref, own_ref, hotg_ref, gext_ref, key_ref, hidt_ref, acc, cold
):
    step = pl.program_id(0)
    w = w_ref[...]
    preact = dot(feat_ref[...], w)
    sigm = jax.nn.sigmoid(preact)
    delta = (up_ref[...].astype(F32) * sigm * (1.0 + preact * (1.0 - sigm))).astype(BF16)
    part = nt_dot(delta, w)

    @pl.when(step == 0)
    def _():
        acc[...] = part
        hidt_ref[...] = hid_ref[...].T
        owner = own_ref[...]
        named = (owner == iota((32, 4 * SAMPLES), 0)).astype(F32)
        before = (iota((256, 256), 0) < iota((256, 256), 1)).astype(BF16)
        carry = jnp.zeros((32, 1), F32)
        ranks = []
        for b in range(4):
            block = named[:, b * 256 : (b + 1) * 256]
            count = dot(block.astype(BF16), before) + carry
            ranks.append(jnp.sum(block * count, axis=0, keepdims=True))
            carry = carry + jnp.sum(block, axis=1, keepdims=True)
        key_ref[...] = owner * 256 + jnp.concatenate(ranks, axis=1).astype(I32)
        row = row_ref[...]
        which = iota((E, 4 * SAMPLES), 0)
        parts = jnp.where(which == 0, row // 128, jnp.where(which == 1, row % 128, 0))
        gext_ref[:, E:] = parts.astype(F32).T.astype(BF16)

    @pl.when(step > 0)
    def _():
        acc[...] += part

    @pl.when(step == pl.num_programs(0) - 1)
    def _():
        for f in range(HOT_FIELDS):
            hotg_ref[f] = acc[:, f * E : (f + 1) * E].astype(BF16)
        for f in range(COLD_FIELDS):
            cold[pl.ds(f, SAMPLES, stride=COLD_FIELDS), :] = acc[:, (HOT_FIELDS + f) * E : (HOT_FIELDS + f + 1) * E]
        gext_ref[:, :E] = cold[...].astype(BF16)


def grads(features, w_in, upstream, hot_ids, cold_rows, owners):
    lookups = SAMPLES * COLD_FIELDS
    fixed = lambda shape: pl.BlockSpec(shape, lambda j: (0,) * len(shape))
    return pl.pallas_call(
        grads_kernel,
        grid=(w_in.shape[1] // STEP,),
        in_specs=[
            fixed(features.shape),
            pl.BlockSpec((w_in.shape[0], STEP), lambda j: (0, j)),
            pl.BlockSpec((SAMPLES, STEP), lambda j: (0, j)),
            fixed(hot_ids.shape),
            fixed((1, lookups)),
            fixed((1, lookups)),
        ],
        out_specs=[
            fixed((HOT_FIELDS, SAMPLES, E)),
            fixed((lookups, 2 * E)),
            fixed((1, lookups)),
            fixed((HOT_FIELDS, SAMPLES)),
        ],
        out_shape=[
            jax.ShapeDtypeStruct((HOT_FIELDS, SAMPLES, E), BF16),
            jax.ShapeDtypeStruct((lookups, 2 * E), BF16),
            jax.ShapeDtypeStruct((1, lookups), I32),
            jax.ShapeDtypeStruct((HOT_FIELDS, SAMPLES), I32),
        ],
        scratch_shapes=[pltpu.VMEM((SAMPLES, w_in.shape[0]), F32), pltpu.VMEM((lookups, E), F32)],
        compiler_params=pltpu.CompilerParams(vmem_limit_bytes=40 << 20),
        name="grads",
    )(features, w_in, upstream, hot_ids, cold_rows, owners)


def sums_kernel(
    gext_ref, key_ref, hotg_ref, hid_ref, cold_ref, hot_ref,
    csend, crecv, hotg2, hid2, hacc, xsend, xrecv, ysend, yown, yrecv, zsend, zrecv, grecv,
    c_ss, c_rs, h_ss, h_rs, x_ss, x_rs, y_ss, y_rs, z_ss, z_rs, g_ss, g_rs,
):
    g, s = lax.axis_index("grp"), lax.axis_index("shard")
    zl, y = g // 8, g % 8
    zh, x, c = s // 8, (s // 2) % 4, s % 2
    z = zh * 4 + zl

    def at(zh, x, c):
        return (zh * 4 + x) * 2 + c

    def cold_peer(k):
        return at((zh + k // 8) % 3, (x + (k // 2) % 4) % 4, (c + k % 2) % 2)

    def y_peer(d):
        return (zl * 8 + (y + d) % 8, s)

    def z_peer(d):
        to = (z + d) % 12
        return ((to % 4) * 8 + y, at(to // 4, x, c))

    def copy(src, dst, ss, rs, peer):
        return pltpu.make_async_remote_copy(
            src_ref=src, dst_ref=dst, send_sem=ss, recv_sem=rs, device_id=peer, device_id_type=MESH
        )

    def cold_copy(k):
        return copy(csend.at[k], crecv.at[k, pl.ds(0, SLOTS)], c_ss.at[k], c_rs.at[k], (g, cold_peer(k)))

    def x_copy(d):
        return copy(xsend.at[d], xrecv.at[d], x_ss.at[d], x_rs.at[d], (g, at(zh, (x + d) % 4, c)))

    def y_copy(d):
        return copy(ysend.at[d], yrecv.at[d], y_ss.at[d], y_rs.at[d], y_peer(d))

    def z_copy(d):
        return copy(zsend.at[((z + d) % 12) // 4], zrecv.at[z], z_ss.at[d], z_rs.at[d], z_peer(d))

    def g_copy(d):
        return copy(grecv.at[y], grecv.at[y], g_ss.at[d], g_rs.at[d], y_peer(d))

    barrier = pltpu.get_barrier_semaphore()

    def greet(peer):
        pl.semaphore_signal(barrier, inc=1, device_id=peer, device_id_type=MESH)

    for k in range(1, OWNERS):
        greet((g, cold_peer(k)))
    for d in range(1, 8):
        greet(y_peer(d))
    for d in range(1, 12):
        if d not in (4, 8):
            greet(z_peer(d))

    which = iota((8, E), 0)
    column = iota((8, E), 1)
    pick = jnp.where(
        ((which == 2) | (which == 3)) & (column == 0) | ((which == 4) | (which == 5)) & (column == 1), 1.0, 0.0
    ).astype(BF16)

    def place(k, carry):
        slot = key_ref[...] - cold_peer(k) * 256
        chosen = (slot == iota((SLOTS, slot.shape[1]), 0)).astype(BF16)
        rows = dot(chosen, gext_ref[...])
        numbers = jnp.concatenate([rows[:, E:], jnp.zeros((DEPTH - SLOTS, E), F32)], axis=0).astype(BF16)
        numbers = nt_dot(pick, numbers)
        tail = jnp.where((which == 2) | (which == 4), numbers[:, :E], numbers[:, E:])
        csend[k] = jnp.concatenate([rows[:HEAD, :E], rows[HEAD:, :E] + tail], axis=0).astype(BF16)
        crecv[k, SLOTS:, :] = jnp.zeros((DEPTH - SLOTS, E), BF16)
        return carry

    lax.fori_loop(0, OWNERS, place, 0)
    crecv[0, :SLOTS, :] = csend[0]
    cold_ref[...] = jnp.zeros_like(cold_ref)
    pl.semaphore_wait(barrier, OWNERS - 1 + 7 + 9)

    hot_pair = copy(hotg_ref, hotg2, h_ss.at[0], h_rs.at[0], (g, at(zh, x, 1 - c)))
    ids_pair = copy(hid_ref, hid2, h_ss.at[1], h_rs.at[1], (g, at(zh, x, 1 - c)))
    ids_pair.start()
    hot_pair.start()

    def send_far(i, carry):
        cold_copy(8 * (1 + i % 2) + i // 2).start()
        return carry

    lax.fori_loop(0, 16, send_far, 0)

    def send_near(k, carry):
        cold_copy(k).start()
        return carry

    lax.fori_loop(1, 8, send_near, 0)

    def hot_block(i, ids_ref, rows_ref):
        base = at(i % 3, (x + i // 3) % 4, c) * 256
        total = jnp.zeros((256, E), F32)
        for f in range(HOT_FIELDS):
            named = (ids_ref[f : f + 1, :] - base == iota((256, SAMPLES), 0)).astype(BF16)
            total = total + dot(named, rows_ref[f])
        return total

    def hot_mine(i, carry):
        hacc[i] = hot_block(i, hid_ref, hotg_ref)
        return carry

    lax.fori_loop(0, 12, hot_mine, 0)
    ids_pair.wait_recv()
    hot_pair.wait_recv()

    def hot_theirs(i, carry):
        xsend[i // 3, pl.ds((i % 3) * 256, 256), :] = (hacc[i] + hot_block(i, hid2, hotg2)).astype(BF16)
        return carry

    for d in (1, 3, 2):
        lax.fori_loop(3 * d, 3 * d + 3, hot_theirs, 0)
        x_copy(d).start()

    def hot_own(i, carry):
        hacc[i] = hacc[i] + hot_block(i, hid2, hotg2)
        return carry

    lax.fori_loop(0, 3, hot_own, 0)

    def cold_add(k, carry):
        tile = crecv[k, SLOTS - 16 : SLOTS, :].astype(F32)
        low = tile[10:11] * 128.0 + tile[12:13]
        high = jnp.where(iota((1, E), 1) < USED - 128, tile[11:12] * 128.0 + tile[13:14], -1.0)
        ids = jnp.concatenate([low, high], axis=1).astype(I32)
        rows = crecv[k]
        for b in range(OWNED // 256):
            named = (ids - b * 256 == iota((256, DEPTH), 0)).astype(BF16)
            cold_ref[b * 256 : (b + 1) * 256, :] += dot(named, rows)
        return carry

    def cold_arrived(k, carry):
        cold_copy(k).wait_recv()
        return cold_add(k, carry)

    cold_add(0, 0)
    lax.fori_loop(1, 8, cold_arrived, 0)

    for d in (1, 3, 2):
        x_copy(d).wait_recv()

    def over_x(i, carry):
        rows = pl.ds(i * 256, 256)
        total = hacc[i]
        for d in range(1, 4):
            total = total + xrecv[d, rows, :].astype(F32)
        hacc[i] = total
        return carry

    lax.fori_loop(0, 3, over_x, 0)

    def to_y(d, carry):
        rows = pl.ds(pl.multiple_of(((y + d) % 8) * 32, 32), 32)
        for i in range(3):
            ysend[d, i * 32 : (i + 1) * 32, :] = hacc[i, rows, :].astype(BF16)
        y_copy(d).start()
        return carry

    lax.fori_loop(1, 8, to_y, 0)
    mine = pl.ds(pl.multiple_of(y * 32, 32), 32)
    for i in range(3):
        yown[i] = hacc[i, mine, :]

    lax.fori_loop(8, 14, cold_arrived, 0)

    for d in range(1, 8):
        y_copy(d).wait_recv()
    for i in range(3):
        total = yown[i]
        for d in range(1, 8):
            total = total + yrecv[d, i * 32 : (i + 1) * 32, :].astype(F32)
        zsend[i] = total
    zrecv[z] = zsend[zh]
    for d in range(1, 12):
        z_copy(d).start()

    lax.fori_loop(14, 19, cold_arrived, 0)

    for d in range(1, 12):
        copy(zsend.at[zh], zrecv.at[(z + 12 - d) % 12], z_ss.at[d], z_rs.at[d], z_peer(d)).wait_recv()
    total = zrecv[0]
    for i in range(1, 12):
        total = total + zrecv[i]
    grecv[y] = total
    for d in range(1, 8):
        g_copy(d).start()

    lax.fori_loop(19, OWNERS, cold_arrived, 0)

    for d in range(1, 8):
        copy(grecv.at[y], grecv.at[(y + 8 - d) % 8], g_ss.at[d], g_rs.at[d], y_peer(d)).wait_recv()
    for i in range(8):
        hot_ref[i * 32 : (i + 1) * 32, :] = grecv[i]

    def cold_sent(k, carry):
        cold_copy(k).wait_send()
        return carry

    lax.fori_loop(1, OWNERS, cold_sent, 0)
    ids_pair.wait_send()
    hot_pair.wait_send()
    for d in range(1, 4):
        x_copy(d).wait_send()
    for d in range(1, 8):
        y_copy(d).wait_send()
        g_copy(d).wait_send()
    for d in range(1, 12):
        z_copy(d).wait_send()


def sums(gext, key, hotg, hid):
    vmem = pl.BlockSpec(memory_space=pltpu.VMEM)
    dma = pltpu.SemaphoreType.DMA
    pairs = lambda n: [dma((n,)), dma((n,))]
    return pl.pallas_call(
        sums_kernel,
        in_specs=[vmem] * 4,
        out_specs=[vmem] * 2,
        out_shape=[jax.ShapeDtypeStruct((OWNED, E), F32), jax.ShapeDtypeStruct((256, E), F32)],
        scratch_shapes=[
            pltpu.VMEM((OWNERS, SLOTS, E), BF16),
            pltpu.VMEM((OWNERS, DEPTH, E), BF16),
            pltpu.VMEM((HOT_FIELDS, SAMPLES, E), BF16),
            pltpu.VMEM((HOT_FIELDS, SAMPLES), I32),
            pltpu.VMEM((12, 256, E), F32),
            pltpu.VMEM((4, 768, E), BF16),
            pltpu.VMEM((4, 768, E), BF16),
            pltpu.VMEM((8, 96, E), BF16),
            pltpu.VMEM((3, 32, E), F32),
            pltpu.VMEM((8, 96, E), BF16),
            pltpu.VMEM((3, 32, E), F32),
            pltpu.VMEM((12, 32, E), F32),
            pltpu.VMEM((8, 32, E), F32),
        ]
        + pairs(OWNERS) + pairs(2) + pairs(4) + pairs(8) + pairs(12) + pairs(8),
        compiler_params=pltpu.CompilerParams(
            collective_id=0, has_side_effects=True, vmem_limit_bytes=40 << 20
        ),
        name="sums",
    )(gext, key, hotg, hid)


def adagrad(rows, accum, grads):
    accum_new = accum + jnp.mean(grads * grads, axis=1)
    return (rows - learn_rate * grads / jnp.sqrt(accum_new)[:, None], accum_new)


def shards(
    features,
    w_in,
    upstream,
    hot_ids,
    cold_rows,
    cold_owner,
    hot_table,
    hot_accum,
    cold_table,
    cold_accum,
):
    hotg, gext, key, hid = grads(
        features, w_in, upstream, hot_ids, cold_rows.reshape(1, -1), cold_owner.reshape(1, -1)
    )
    cold_sum, hot_sum = sums(gext, key, hotg, hid)
    hot_new, hot_accum_new = adagrad(hot_table, hot_accum, hot_sum)
    cold_new, cold_accum_new = adagrad(cold_table, cold_accum, cold_sum)
    return (hot_new, hot_accum_new, cold_new, cold_accum_new)


def solution(mesh):
    placed = (
        P(("grp", "shard"), None),
        P(),
        P(("grp", "shard"), None),
        P(("grp", "shard"), None),
        P(("grp", "shard")),
        P(("grp", "shard"), None),
        P("shard", None),
        P("shard"),
        P(("grp", "shard"), None),
        P(("grp", "shard")),
    )
    return jax.shard_map(
        shards,
        mesh=mesh,
        in_specs=placed,
        out_specs=(P("shard", None), P("shard"), P(("grp", "shard"), None), P(("grp", "shard"))),
        check_vma=False,
    )
```

```python
import jax
import jax.numpy as jnp
from jax import lax
from jax.experimental import pallas as pl
from jax.experimental.pallas import tpu as pltpu
from jax.sharding import PartitionSpec as P

MESH = pl.DeviceIdType.MESH
learn_rate = 0.5

E = 128
SAMPLES = 256
HOT_FIELDS, COLD_FIELDS = 8, 4
PLANE = 8
LOOKUPS = 1024
SLOTS = 176
USED = 170
HEAD = 168
DEPTH = 256
OWNED = 2048
STEP = 256
STEPS = 4
BF16, F32, I32 = jnp.bfloat16, jnp.float32, jnp.int32


def iota(shape, axis):
    return lax.broadcasted_iota(I32, shape, axis)


def nt_dot(a, b):
    return lax.dot_general(a, b, (((1,), (1,)), ((), ())), preferred_element_type=F32)


def dot(a, b):
    return jnp.dot(a, b, preferred_element_type=F32)


def step_kernel(
    feat_hbm, w_hbm, up_hbm, hid_ref, row_ref, own_ref, cold_ref, hot_ref,
    feat, w, up, delta, hotg, hotg2, hid2, wide, hacc, xsend, xrecv, ysend, yown, yrecv, zsend, zrecv, grecv,
    raw, packed, loose, csend, crecv,
    l_s, r_ss, r_rs, p_ss, p_rs, c_ss, c_rs, h_ss, h_rs, x_ss, x_rs, y_ss, y_rs, z_ss, z_rs, g_ss, g_rs,
):
    g, s = lax.axis_index("grp"), lax.axis_index("shard")
    zl, y = g // 8, g % 8
    zh, x, c = s // 8, (s // 2) % 4, s % 2
    z = zh * 4 + zl

    def at(zh, x, c):
        return (zh * 4 + x) * 2 + c

    def plane_peer(k):
        return (g, at(zh, (x + k // 2) % 4, (c + k % 2) % 2))

    def y_peer(d):
        return (zl * 8 + (y + d) % 8, s)

    def z_peer(d):
        to = (z + d) % 12
        return ((to % 4) * 8 + y, at(to // 4, x, c))

    def copy(src, dst, ss, rs, peer):
        return pltpu.make_async_remote_copy(
            src_ref=src, dst_ref=dst, send_sem=ss, recv_sem=rs, device_id=peer, device_id_type=MESH
        )

    def raw_copy(q):
        return copy(raw.at[0], raw.at[q], r_ss.at[q], r_rs.at[q], (g, at((zh + q) % 3, x, c)))

    def packed_copy(q):
        return copy(packed.at[0], packed.at[q], p_ss.at[q], p_rs.at[q], (g, at((zh + q) % 3, x, c)))

    def cold_copy(q, k):
        return copy(
            csend.at[q, k], crecv.at[q, k, pl.ds(0, SLOTS)], c_ss.at[q, k], c_rs.at[q, k], plane_peer(k)
        )

    def pair_copy(i):
        return copy(
            hotg.at[pl.ds(2 * i, 2)], hotg2.at[pl.ds(2 * i, 2)], h_ss.at[i], h_rs.at[i], plane_peer(1)
        )

    ids_copy = copy(hid_ref, hid2, h_ss.at[4], h_rs.at[4], plane_peer(1))

    def x_copy(d):
        return copy(xsend.at[d], xrecv.at[d], x_ss.at[d], x_rs.at[d], plane_peer(2 * d))

    def y_copy(d):
        return copy(ysend.at[d], yrecv.at[d], y_ss.at[d], y_rs.at[d], y_peer(d))

    def z_copy(d):
        return copy(zsend.at[((z + d) % 12) // 4], zrecv.at[z], z_ss.at[d], z_rs.at[d], z_peer(d))

    def g_copy(d):
        return copy(grecv.at[y], grecv.at[y], g_ss.at[d], g_rs.at[d], y_peer(d))

    barrier = pltpu.get_barrier_semaphore()

    def greet(peer):
        pl.semaphore_signal(barrier, inc=1, device_id=peer, device_id_type=MESH)

    for d in (4, 8, 1, 2, 3, 5, 6, 7, 9, 10, 11):
        greet(z_peer(d))
    for k in range(1, PLANE):
        greet(plane_peer(k))
    for d in range(1, 8):
        greet(y_peer(d))

    feat_copy = pltpu.make_async_copy(feat_hbm, feat, l_s.at[STEPS])
    up_copy = pltpu.make_async_copy(up_hbm, up, l_s.at[STEPS + 1])

    def w_copy(j):
        columns = pl.ds(pl.multiple_of(j * STEP, STEP), STEP)
        return pltpu.make_async_copy(w_hbm.at[:, columns], w.at[j], l_s.at[j])

    feat_copy.start()
    w_copy(0).start()
    up_copy.start()
    for j in range(1, STEPS):
        w_copy(j).start()

    owner = own_ref[...]
    named = (owner == iota((32, LOOKUPS), 0)).astype(F32)
    before = (iota((256, 256), 0) < iota((256, 256), 1)).astype(BF16)
    carry = jnp.zeros((32, 1), F32)
    ranks = []
    for b in range(LOOKUPS // 256):
        block = named[:, b * 256 : (b + 1) * 256]
        count = dot(block.astype(BF16), before) + carry
        ranks.append(jnp.sum(block * count, axis=0, keepdims=True))
        carry = carry + jnp.sum(block, axis=1, keepdims=True)
    packed[0] = (owner * 256 + jnp.concatenate(ranks, axis=1).astype(I32)) * OWNED + row_ref[...]
    crecv[:, :, SLOTS:, :] = jnp.zeros((3, PLANE, DEPTH - SLOTS, E), BF16)
    cold_ref[...] = jnp.zeros_like(cold_ref)
    hacc[...] = jnp.zeros_like(hacc)

    feat_copy.wait()

    def grad_step(j, total):
        w_copy(j).wait()
        preact = dot(feat[...], w[j])
        sigm = jax.nn.sigmoid(preact)
        part = (up[:, pl.ds(pl.multiple_of(j * STEP, STEP), STEP)].astype(F32) * sigm * (1.0 + preact * (1.0 - sigm))).astype(BF16)
        delta[j] = part
        return total + nt_dot(part, w[j, HOT_FIELDS * E :, :])

    up_copy.wait()
    total = lax.fori_loop(0, STEPS, grad_step, jnp.zeros((SAMPLES, COLD_FIELDS * E), F32))
    for f in range(COLD_FIELDS):
        loose[pl.ds(f, SAMPLES, stride=COLD_FIELDS), :] = total[:, f * E : (f + 1) * E]
    raw[0] = loose[...].astype(BF16)

    pl.semaphore_wait(barrier, 11 + 7 + 7)
    for q in (1, 2):
        raw_copy(q).start()
        packed_copy(q).start()
    ids_copy.start()

    def hot_step(i, carry):
        rows = pl.ds(pl.multiple_of(i * 2 * E, 2 * E), 2 * E)
        total = nt_dot(delta[0], w[0, rows, :])
        for j in range(1, STEPS):
            total = total + nt_dot(delta[j], w[j, rows, :])
        hotg[2 * i] = total[:, :E].astype(BF16)
        hotg[2 * i + 1] = total[:, E:].astype(BF16)
        pair_copy(i).start()
        return carry

    lax.fori_loop(0, HOT_FIELDS // 2, hot_step, 0)

    def hot_add(ids_ref, rows_ref, parity):
        ids = ids_ref[...]
        place = ids // 256
        away = ((place // 2) % 4 - x + 4) % 4
        inside = (place % 2 == c) & (away % 2 == parity)
        spot = jnp.where(inside, place // 8 * 256 + ids % 256, -1)
        for i in range(HOT_FIELDS // 2):
            chosen = jnp.concatenate(
                [(spot[2 * i + n : 2 * i + n + 1, :] == iota((768, SAMPLES), 0)).astype(BF16) for n in range(2)], axis=1
            )
            hacc[parity] += dot(chosen, rows_ref[2 * i * SAMPLES : (2 * i + 2) * SAMPLES, :])

    def widen(ids_ref, rows_ref):
        far = ((ids_ref[...] // 512) % 4 - x + 4) % 4 // 2
        far = far.astype(F32).T
        for f in range(HOT_FIELDS):
            keep = jnp.broadcast_to(far[:, f : f + 1], (SAMPLES, E)).astype(BF16)
            rows = rows_ref[f]
            second = rows * keep
            wide[f * SAMPLES : (f + 1) * SAMPLES, :E] = rows - second
            wide[f * SAMPLES : (f + 1) * SAMPLES, E:] = second

    widen(hid_ref, hotg)
    hot_add(hid_ref, wide, 1)
    hot_add(hid_ref, wide, 0)
    ids_copy.wait_recv()
    for i in range(HOT_FIELDS // 2):
        pair_copy(i).wait_recv()
    widen(hid2, hotg2)
    hot_add(hid2, wide, 1)
    xsend[1] = hacc[1, :, :E].astype(BF16)
    x_copy(1).start()
    xsend[3] = hacc[1, :, E:].astype(BF16)
    x_copy(3).start()
    hot_add(hid2, wide, 0)
    xsend[2] = hacc[0, :, E:].astype(BF16)
    x_copy(2).start()

    which = iota((8, E), 0)
    column = iota((8, E), 1)
    pick = jnp.where(
        ((which == 2) | (which == 3)) & (column == 0) | ((which == 4) | (which == 5)) & (column == 1), 1.0, 0.0
    ).astype(BF16)

    def place(q):
        both = packed[q]
        slot, row = both // OWNED, both % OWNED
        sort = iota((E, LOOKUPS), 0)
        parts = jnp.where(sort == 0, row // 128, jnp.where(sort == 1, row % 128, 0)).astype(F32).T
        rows = jnp.concatenate([raw[q], parts.astype(BF16)], axis=1)

        def pair(dx):
            base = slot - at(zh, (x + dx) % 4, 0) * 256
            chosen = jnp.concatenate(
                [(base - n * 256 == iota((SLOTS, LOOKUPS), 0)).astype(BF16) for n in range(2)], axis=0
            )
            placed = dot(chosen, rows)
            for n in range(2):
                half = placed[n * SLOTS : (n + 1) * SLOTS]
                numbers = jnp.concatenate([half[:, E:], jnp.zeros((DEPTH - SLOTS, E), F32)], axis=0).astype(BF16)
                numbers = nt_dot(pick, numbers)
                tail = jnp.where((which == 2) | (which == 4), numbers[:, :E], numbers[:, E:])
                k = 2 * dx + (n + c) % 2
                csend[q, k] = jnp.concatenate([half[:HEAD, :E], half[HEAD:, :E] + tail], axis=0).astype(BF16)

        def far(dx, carry):
            pair(dx)
            cold_copy(q, 2 * dx).start()
            cold_copy(q, 2 * dx + 1).start()
            return carry

        lax.fori_loop(1, 4, far, 0)
        pair(0)
        cold_copy(q, 1).start()
        crecv[q, 0, :SLOTS, :] = csend[q, 0]

    def cold_add(q, ks):
        ids, rows = [], []
        for k in ks:
            tile = crecv[q, k, SLOTS - 16 : SLOTS, :].astype(F32)
            low = tile[10:11] * 128.0 + tile[12:13]
            high = jnp.where(iota((1, E), 1) < USED - 128, tile[11:12] * 128.0 + tile[13:14], -1.0)
            number = jnp.concatenate([low, high], axis=1)
            far = jnp.broadcast_to((number >= OWNED // 2).astype(F32), (8, DEPTH)).T
            keep = jnp.broadcast_to(far[:, :1], (DEPTH, E)).astype(BF16)
            arrived = crecv[q, k]
            second = arrived * keep
            rows.append(jnp.concatenate([arrived - second, second], axis=1))
            ids.append(number.astype(I32))
        ids, rows = jnp.concatenate(ids, axis=1), jnp.concatenate(rows, axis=0)
        ids = jnp.where(ids < 0, -1, ids % (OWNED // 2))
        for b in range(OWNED // 512):
            chosen = (ids - b * 256 == iota((256, ids.shape[1]), 0)).astype(BF16)
            total = dot(chosen, rows)
            cold_ref[b * 256 : (b + 1) * 256, :] += total[:, :E]
            cold_ref[OWNED // 2 + b * 256 : OWNED // 2 + (b + 1) * 256, :] += total[:, E:]

    def cold_arrived(q):
        def step(i, carry):
            cold_copy(q, 2 * i).wait_recv()
            cold_copy(q, 2 * i + 1).wait_recv()
            cold_add(q, (2 * i, 2 * i + 1))
            return carry

        cold_copy(q, 1).wait_recv()
        cold_add(q, (0, 1))
        lax.fori_loop(1, 4, step, 0)

    place(0)

    for d in (1, 3, 2):
        x_copy(d).wait_recv()

    def over_x(i, carry):
        rows = pl.ds(pl.multiple_of(i * 256, 256), 256)
        total = hacc[0, rows, :E]
        for d in range(1, 4):
            total = total + xrecv[d, rows, :].astype(F32)
        hacc[0, rows, :E] = total
        return carry

    lax.fori_loop(0, 3, over_x, 0)

    def to_y(d, carry):
        for i in range(3):
            rows = pl.ds(pl.multiple_of(((y + d) % 8) * 32 + i * 256, 32), 32)
            ysend[d, i * 32 : (i + 1) * 32, :] = hacc[0, rows, :E].astype(BF16)
        y_copy(d).start()
        return carry

    lax.fori_loop(1, 8, to_y, 0)
    for i in range(3):
        yown[i] = hacc[0, pl.ds(pl.multiple_of(y * 32 + i * 256, 32), 32), :E]

    cold_arrived(0)

    for d in range(1, 8):
        y_copy(d).wait_recv()
    for i in range(3):
        total = yown[i]
        for d in range(1, 8):
            total = total + yrecv[d, i * 32 : (i + 1) * 32, :].astype(F32)
        zsend[i] = total
    zrecv[z] = zsend[zh]
    for d in range(1, 12):
        z_copy(d).start()

    for q in (1, 2):
        packed_copy(q).wait_recv()
        raw_copy(q).wait_recv()
        place(q)

    for d in range(1, 12):
        copy(zsend.at[zh], zrecv.at[(z + 12 - d) % 12], z_ss.at[d], z_rs.at[d], z_peer(d)).wait_recv()
    total = zrecv[0]
    for i in range(1, 12):
        total = total + zrecv[i]
    grecv[y] = total
    for d in range(1, 8):
        g_copy(d).start()

    cold_arrived(1)
    cold_arrived(2)

    for d in range(1, 8):
        copy(grecv.at[y], grecv.at[(y + 8 - d) % 8], g_ss.at[d], g_rs.at[d], y_peer(d)).wait_recv()
    for i in range(8):
        hot_ref[i * 32 : (i + 1) * 32, :] = grecv[i]

    for q in (1, 2):
        raw_copy(q).wait_send()
        packed_copy(q).wait_send()
    ids_copy.wait_send()
    for i in range(HOT_FIELDS // 2):
        pair_copy(i).wait_send()

    def cold_sent(k, carry):
        for q in range(3):
            cold_copy(q, k).wait_send()
        return carry

    lax.fori_loop(1, PLANE, cold_sent, 0)
    for d in range(1, 4):
        x_copy(d).wait_send()
    for d in range(1, 8):
        y_copy(d).wait_send()
        g_copy(d).wait_send()
    for d in range(1, 12):
        z_copy(d).wait_send()


def step(features, w_in, upstream, hot_ids, cold_rows, owners):
    vmem = pl.BlockSpec(memory_space=pltpu.VMEM)
    hbm = pl.BlockSpec(memory_space=pl.ANY)
    dma = pltpu.SemaphoreType.DMA
    pairs = lambda *n: [dma(n), dma(n)]
    return pl.pallas_call(
        step_kernel,
        in_specs=[hbm] * 3 + [vmem] * 3,
        out_specs=[vmem] * 2,
        out_shape=[jax.ShapeDtypeStruct((OWNED, E), F32), jax.ShapeDtypeStruct((256, E), F32)],
        scratch_shapes=[
            pltpu.VMEM(features.shape, BF16),
            pltpu.VMEM((STEPS, w_in.shape[0], STEP), BF16),
            pltpu.VMEM(upstream.shape, BF16),
            pltpu.VMEM((STEPS, SAMPLES, STEP), BF16),
            pltpu.VMEM((HOT_FIELDS, SAMPLES, E), BF16),
            pltpu.VMEM((HOT_FIELDS, SAMPLES, E), BF16),
            pltpu.VMEM((HOT_FIELDS, SAMPLES), I32),
            pltpu.VMEM((HOT_FIELDS * SAMPLES, 2 * E), BF16),
            pltpu.VMEM((2, 768, 2 * E), F32),
            pltpu.VMEM((4, 768, E), BF16),
            pltpu.VMEM((4, 768, E), BF16),
            pltpu.VMEM((8, 96, E), BF16),
            pltpu.VMEM((3, 32, E), F32),
            pltpu.VMEM((8, 96, E), BF16),
            pltpu.VMEM((3, 32, E), F32),
            pltpu.VMEM((12, 32, E), F32),
            pltpu.VMEM((8, 32, E), F32),
            pltpu.VMEM((3, LOOKUPS, E), BF16),
            pltpu.VMEM((3, 1, LOOKUPS), I32),
            pltpu.VMEM((LOOKUPS, E), F32),
            pltpu.VMEM((3, PLANE, SLOTS, E), BF16),
            pltpu.VMEM((3, PLANE, DEPTH, E), BF16),
            dma((STEPS + 2,)),
        ]
        + pairs(3) + pairs(3) + pairs(3, PLANE) + pairs(5) + pairs(4) + pairs(8) + pairs(12) + pairs(8),
        compiler_params=pltpu.CompilerParams(
            collective_id=0, has_side_effects=True, vmem_limit_bytes=56 << 20
        ),
        name="step",
    )(features, w_in, upstream, hot_ids, cold_rows, owners)


def adagrad(rows, accum, grads):
    accum_new = accum + jnp.mean(grads * grads, axis=1)
    return (rows - learn_rate * grads / jnp.sqrt(accum_new)[:, None], accum_new)


def shards(
    features,
    w_in,
    upstream,
    hot_ids,
    cold_rows,
    cold_owner,
    hot_table,
    hot_accum,
    cold_table,
    cold_accum,
):
    cold_sum, hot_sum = step(
        features, w_in, upstream, hot_ids.T, cold_rows.reshape(1, -1), cold_owner.reshape(1, -1)
    )
    hot_new, hot_accum_new = adagrad(hot_table, hot_accum, hot_sum)
    cold_new, cold_accum_new = adagrad(cold_table, cold_accum, cold_sum)
    return (hot_new, hot_accum_new, cold_new, cold_accum_new)


def solution(mesh):
    placed = (
        P(("grp", "shard"), None),
        P(),
        P(("grp", "shard"), None),
        P(("grp", "shard"), None),
        P(("grp", "shard")),
        P(("grp", "shard"), None),
        P("shard", None),
        P("shard"),
        P(("grp", "shard"), None),
        P(("grp", "shard")),
    )
    return jax.shard_map(
        shards,
        mesh=mesh,
        in_specs=placed,
        out_specs=(P("shard", None), P("shard"), P(("grp", "shard"), None), P(("grp", "shard"))),
        check_vma=False,
    )
```

```python
import jax
import jax.numpy as jnp
from jax import lax
from jax.experimental import pallas as pl
from jax.experimental.pallas import tpu as pltpu
from jax.sharding import PartitionSpec as P

MESH = pl.DeviceIdType.MESH
learn_rate = 0.5

E = 128
SAMPLES = 256
HOT_FIELDS, COLD_FIELDS = 8, 4
PLANE = 8
LOOKUPS = 1024
SLOTS = 96
USED = 85
HEAD = 88
DEPTH = 128
HALF = 512
OWNED = 2048
STEPS = 3
BLOCK = 512
PARTS = 4
BF16, F32, I32 = jnp.bfloat16, jnp.float32, jnp.int32


def iota(shape, axis):
    return lax.broadcasted_iota(I32, shape, axis)


def nt_dot(a, b):
    return lax.dot_general(a, b, (((1,), (1,)), ((), ())), preferred_element_type=F32)


def dot(a, b):
    return jnp.dot(a, b, preferred_element_type=F32)


def step_kernel(
    feat_hbm, w_hbm, up_hbm, ctab_hbm, htab_hbm, hid_hbm, row_hbm, own_hbm, cacc_hbm, hacc_hbm,
    hot_hbm, hot_accum_hbm, cold_hbm, cold_accum_hbm,
    feat, w, up, hid_ref, row_ref, own_ref, cacc_ref, hacc_ref, pre, delta, order, hotg, hotg2, hid2, wide, hacc, xsend, xrecv, ysend, yown, yrecv, zsend, zrecv, grecv,
    raw, packed, loose, parts, csend, crecv, csum, hsum, ctab, htab, cwas, hwas, cnow, hnow,
    l_s, r_ss, r_rs, p_ss, p_rs, c_ss, c_rs, h_ss, h_rs, x_ss, x_rs, y_ss, y_rs, z_ss, z_rs, g_ss, g_rs,
):
    g, s = lax.axis_index("grp"), lax.axis_index("shard")
    zl, y = g // 8, g % 8
    zh, x, c = s // 8, (s // 2) % 4, s % 2
    z = zh * 4 + zl

    def at(zh, x, c):
        return (zh * 4 + x) * 2 + c

    def plane_peer(k):
        return (g, at(zh, (x + k // 2) % 4, (c + k % 2) % 2))

    def y_peer(d):
        return (zl * 8 + (y + d) % 8, s)

    def z_peer(d):
        to = (z + d) % 12
        return ((to % 4) * 8 + y, at(to // 4, x, c))

    def copy(src, dst, ss, rs, peer):
        return pltpu.make_async_remote_copy(
            src_ref=src, dst_ref=dst, send_sem=ss, recv_sem=rs, device_id=peer, device_id_type=MESH
        )

    def raw_copy(q, h):
        rows = pl.ds(h * HALF, HALF)
        return copy(raw.at[0, rows], raw.at[q, rows], r_ss.at[q, h], r_rs.at[q, h], (g, at((zh + q) % 3, x, c)))

    def packed_copy(q):
        return copy(packed.at[0], packed.at[q], p_ss.at[q], p_rs.at[q], (g, at((zh + q) % 3, x, c)))

    def cold_copy(q, h, k):
        return copy(
            csend.at[q, h, k], crecv.at[q, h, k, pl.ds(0, SLOTS)], c_ss.at[q, h, k], c_rs.at[q, h, k], plane_peer(k)
        )

    def pair_copy(i):
        return copy(
            hotg.at[pl.ds(2 * i, 2)], hotg2.at[pl.ds(2 * i, 2)], h_ss.at[i], h_rs.at[i], plane_peer(1)
        )

    ids_copy = copy(hid_ref, hid2, h_ss.at[4], h_rs.at[4], plane_peer(1))

    def x_copy(d):
        return copy(xsend.at[d], xrecv.at[d], x_ss.at[d], x_rs.at[d], plane_peer(2 * d))

    def y_copy(d):
        return copy(ysend.at[d], yrecv.at[d], y_ss.at[d], y_rs.at[d], y_peer(d))

    def z_copy(d):
        return copy(zsend.at[((z + d) % 12) // 4], zrecv.at[z], z_ss.at[d], z_rs.at[d], z_peer(d))

    def g_copy(d):
        return copy(grecv.at[y], grecv.at[y], g_ss.at[d], g_rs.at[d], y_peer(d))

    def load(src, dst, i):
        return pltpu.make_async_copy(src, dst, l_s.at[i])

    def w_copy(j):
        rows = pl.ds(pl.multiple_of(j * BLOCK, BLOCK), BLOCK)
        return load(w_hbm.at[rows], w.at[rows], j)

    own_copy, row_copy = load(own_hbm, own_ref, STEPS), load(row_hbm, row_ref, STEPS + 1)
    feat_copy, up_copy, hid_copy = (
        load(feat_hbm, feat, STEPS + 2), load(up_hbm, up, STEPS + 3), load(hid_hbm, hid_ref, STEPS + 4)
    )
    late_copies = (
        load(cacc_hbm, cacc_ref, STEPS + 5),
        load(hacc_hbm, hacc_ref, STEPS + 6),
        load(ctab_hbm, ctab, STEPS + 7),
        load(htab_hbm, htab, STEPS + 8),
    )
    cold_out, cold_accum_out = load(ctab, cold_hbm, STEPS + 9), load(cnow, cold_accum_hbm, STEPS + 10)
    hot_out, hot_accum_out = load(htab, hot_hbm, STEPS + 11), load(hnow, hot_accum_hbm, STEPS + 12)
    own_copy.start()
    row_copy.start()
    feat_copy.start()
    for j in range(STEPS):
        w_copy(j).start()
    up_copy.start()
    hid_copy.start()
    for late in late_copies:
        late.start()

    barrier = pltpu.get_barrier_semaphore()

    def greet(peer):
        pl.semaphore_signal(barrier, inc=1, device_id=peer, device_id_type=MESH)

    for d in (4, 8, 1, 2, 3, 5, 6, 7, 9, 10, 11):
        greet(z_peer(d))
    for k in range(1, PLANE):
        greet(plane_peer(k))
    for d in range(1, 8):
        greet(y_peer(d))

    crecv[:, :, :, SLOTS:, :] = jnp.zeros((3, 2, PLANE, DEPTH - SLOTS, E), BF16)
    csum[...] = jnp.zeros_like(csum)
    hacc[...] = jnp.zeros_like(hacc)
    pre[...] = jnp.zeros_like(pre)

    own_copy.wait()
    row_copy.wait()
    owner = own_ref[...]
    named = (owner == iota((32, LOOKUPS), 0)).astype(F32)
    before = (iota((256, 256), 0) < iota((256, 256), 1)).astype(BF16)
    carry = jnp.zeros((32, 1), F32)
    ranks = []
    for b in range(LOOKUPS // 256):
        block = named[:, b * 256 : (b + 1) * 256]
        count = dot(block.astype(BF16), before) + carry
        ranks.append(jnp.sum(block * count, axis=0, keepdims=True))
        carry = carry + jnp.sum(block, axis=1, keepdims=True)
    rank = jnp.concatenate(ranks, axis=1).astype(I32)
    first = jnp.sum(jnp.where(iota((32, LOOKUPS), 0) < owner, carry, 0.0), axis=0, keepdims=True).astype(I32)
    spot = first + rank
    spot = spot % 2 * HALF + spot // 2
    for h in range(2):
        order[h] = (spot - h * HALF == iota((HALF, LOOKUPS), 0)).astype(BF16)
    digit = iota((8, LOOKUPS), 0)
    row = row_ref[...]
    digits = jnp.where(digit == 0, owner, jnp.where(digit == 1, rank // 2, jnp.where(digit == 2, row // 128, row % 128)))
    digits = jnp.where(digit < 4, digits, 0).astype(F32).astype(BF16)

    feat_copy.wait()

    def preact_step(j, carry):
        w_copy(j).wait()
        columns = pl.ds(pl.multiple_of(j * BLOCK, BLOCK), BLOCK)
        pre[...] += dot(feat[:, columns], w[columns, :])
        return carry

    lax.fori_loop(0, STEPS, preact_step, 0)
    up_copy.wait()
    preact = pre[...]
    sigm = jax.nn.sigmoid(preact)
    delta[...] = (up[...].astype(F32) * sigm * (1.0 + preact * (1.0 - sigm))).astype(BF16)
    total = nt_dot(delta[...], w[HOT_FIELDS * E :, :])
    for f in range(COLD_FIELDS):
        loose[pl.ds(f, SAMPLES, stride=COLD_FIELDS), :] = total[:, f * E : (f + 1) * E]
    cold_rows = loose[...].astype(BF16)

    pl.semaphore_wait(barrier, 11 + 7 + 7)
    for h in range(2):
        raw[0, h * HALF : (h + 1) * HALF, :] = dot(order[h], cold_rows).astype(BF16)
    for q in (1, 2):
        raw_copy(q, 0).start()
    hid_copy.wait()
    ids_copy.start()

    def hot_step(i, carry):
        rows = pl.ds(pl.multiple_of(i * 2 * E, 2 * E), 2 * E)
        total = nt_dot(delta[...], w[rows, :])
        hotg[2 * i] = total[:, :E].astype(BF16)
        hotg[2 * i + 1] = total[:, E:].astype(BF16)
        pair_copy(i).start()
        return carry

    lax.fori_loop(0, HOT_FIELDS // 2, hot_step, 0)

    for h in range(2):
        sent = nt_dot(digits, order[h]).astype(I32)
        packed[0, :, h * HALF : (h + 1) * HALF] = ((sent[0:1] * 128 + sent[1:2]) * 16 + sent[2:3]) * 128 + sent[3:4]
    for q in (1, 2):
        packed_copy(q).start()

    def hot_add(ids_ref, which, parity):
        ids = ids_ref[...]
        place = ids // 256
        away = ((place // 2) % 4 - x + 4) % 4
        inside = (place % 2 == c) & (away % 2 == parity)
        spot = jnp.where(inside, place // 8 * 256 + ids % 256, -1)
        for i in range(HOT_FIELDS // 2):
            chosen = jnp.concatenate(
                [(spot[2 * i + n : 2 * i + n + 1, :] == iota((768, SAMPLES), 0)).astype(BF16) for n in range(2)], axis=1
            )
            hacc[parity] += dot(chosen, wide[which, 2 * i * SAMPLES : (2 * i + 2) * SAMPLES, :])

    def widen(ids_ref, rows_ref, which):
        far = ((ids_ref[...] // 512) % 4 - x + 4) % 4 // 2
        far = far.astype(F32).T
        for f in range(HOT_FIELDS):
            keep = jnp.broadcast_to(far[:, f : f + 1], (SAMPLES, E)).astype(BF16)
            rows = rows_ref[f]
            second = rows * keep
            wide[which, f * SAMPLES : (f + 1) * SAMPLES, :E] = rows - second
            wide[which, f * SAMPLES : (f + 1) * SAMPLES, E:] = second

    widen(hid_ref, hotg, 0)
    hot_add(hid_ref, 0, 1)
    ids_copy.wait_recv()
    for i in range(HOT_FIELDS // 2):
        pair_copy(i).wait_recv()
    widen(hid2, hotg2, 1)
    hot_add(hid2, 1, 1)
    xsend[1] = hacc[1, :, :E].astype(BF16)
    x_copy(1).start()
    xsend[3] = hacc[1, :, E:].astype(BF16)
    x_copy(3).start()
    hot_add(hid_ref, 0, 0)
    hot_add(hid2, 1, 0)
    xsend[2] = hacc[0, :, E:].astype(BF16)
    x_copy(2).start()

    which = iota((8, E), 0)
    column = iota((8, E), 1)
    pick = jnp.where(
        (which == 0) & (column == 0) | (which == 1) & (column == 1), 1.0, 0.0
    ).astype(BF16)

    def number(q):
        row = packed[q] % OWNED
        sort = iota((E, LOOKUPS), 0)
        parts[q] = jnp.where(sort == 0, row // 128, jnp.where(sort == 1, row % 128, 0)).astype(F32).T.astype(BF16)

    def place(q, h):
        rows = pl.ds(h * HALF, HALF)
        held = jnp.concatenate([raw[q, rows, :], parts[q, rows, :]], axis=1)
        slot = packed[q, :, rows] // OWNED - at(zh, 0, 0) * DEPTH
        for b in range(2):
            chosen = (slot - b * 4 * DEPTH == iota((4 * DEPTH, HALF), 0)).astype(BF16)
            filled = dot(chosen, held)
            numbers = nt_dot(pick, filled[:, E:].astype(BF16))
            for n in range(4):
                to = b * 4 + n
                half = filled[n * DEPTH : n * DEPTH + SLOTS, :E]
                tail = half[HEAD:] + numbers[:, n * DEPTH : (n + 1) * DEPTH]
                k = (to // 2 - x + 4) % 4 * 2 + (to % 2 - c + 2) % 2
                csend[q, h, k] = jnp.concatenate([half[:HEAD], tail], axis=0).astype(BF16)

        def send(k, carry):
            cold_copy(q, h, k).start()
            return carry

        lax.fori_loop(1, PLANE, send, 0)
        crecv[q, h, 0, :SLOTS, :] = csend[q, h, 0]

    def cold_add(q, h, ks):
        ids, rows = [], []
        for k in ks:
            tile = crecv[q, h, k, SLOTS - 16 : SLOTS, :].astype(F32)
            row = jnp.where(iota((1, E), 1) < USED, tile[8:9] * 128.0 + tile[9:10], -1.0)
            far = jnp.broadcast_to((row >= OWNED // 2).astype(F32), (8, DEPTH)).T
            keep = jnp.broadcast_to(far[:, :1], (DEPTH, E)).astype(BF16)
            arrived = crecv[q, h, k]
            second = arrived * keep
            rows.append(jnp.concatenate([arrived - second, second], axis=1))
            ids.append(row.astype(I32))
        ids, rows = jnp.concatenate(ids, axis=1), jnp.concatenate(rows, axis=0)
        ids = jnp.where(ids < 0, -1, ids % (OWNED // 2))
        for b in range(OWNED // 512):
            chosen = (ids - b * 256 == iota((256, ids.shape[1]), 0)).astype(BF16)
            total = dot(chosen, rows)
            csum[b * 256 : (b + 1) * 256, :] += total[:, :E]
            csum[OWNED // 2 + b * 256 : OWNED // 2 + (b + 1) * 256, :] += total[:, E:]

    def cold_arrived(q, h):
        for k in range(1, 4):
            cold_copy(q, h, k).wait_recv()
        cold_add(q, h, range(4))
        for k in range(4, 8):
            cold_copy(q, h, k).wait_recv()
        cold_add(q, h, range(4, 8))

    def spread(was, accum_ref):
        def block(b, carry):
            rows = pl.ds(pl.multiple_of(b * E, E), E)
            was[rows, :] = jnp.broadcast_to(accum_ref[pl.ds(b, 1), :], (E, E)).T
            return carry

        lax.fori_loop(0, accum_ref.shape[0], block, 0)

    def adagrad(sum_ref, table, was, now_ref):
        ones = jnp.ones((2 * E, E), BF16)
        corner = iota((E, E), 0) == iota((E, E), 1)

        def block(b, carry):
            rows = pl.ds(pl.multiple_of(b * E, E), E)
            grads = sum_ref[rows, :]
            square = grads * grads
            high = square.astype(BF16)
            low = (square - high.astype(F32)).astype(BF16)
            now = was[rows, :] + dot(jnp.concatenate([high, low], axis=1), ones) * (1.0 / E)
            table[rows, :] = table[rows, :] - learn_rate * grads / jnp.sqrt(now)
            now_ref[pl.ds(b, 1), :] = jnp.sum(jnp.where(corner, now, 0.0), axis=0, keepdims=True)
            return carry

        lax.fori_loop(0, now_ref.shape[0], block, 0)

    number(0)
    place(0, 0)
    place(0, 1)
    for q in (1, 2):
        raw_copy(q, 0).wait_send()
        raw_copy(q, 1).start()
    for late in late_copies:
        late.wait()
    spread(cwas, cacc_ref)
    spread(hwas, hacc_ref)

    for d in (1, 3, 2):
        x_copy(d).wait_recv()

    def over_x(i, carry):
        rows = pl.ds(pl.multiple_of(i * 256, 256), 256)
        total = hacc[0, rows, :E]
        for d in range(1, 4):
            total = total + xrecv[d, rows, :].astype(F32)
        hacc[0, rows, :E] = total
        return carry

    lax.fori_loop(0, 3, over_x, 0)

    def to_y(d, carry):
        for i in range(3):
            rows = pl.ds(pl.multiple_of(((y + d) % 8) * 32 + i * 256, 32), 32)
            ysend[d, i * 32 : (i + 1) * 32, :] = hacc[0, rows, :E].astype(BF16)
        y_copy(d).start()
        return carry

    lax.fori_loop(1, 8, to_y, 0)
    for i in range(3):
        yown[i] = hacc[0, pl.ds(pl.multiple_of(y * 32 + i * 256, 32), 32), :E]

    cold_arrived(0, 0)
    cold_arrived(0, 1)
    for q in (1, 2):
        packed_copy(q).wait_recv()
        number(q)
    for q in (1, 2):
        raw_copy(q, 0).wait_recv()
        place(q, 0)

    for d in range(1, 8):
        y_copy(d).wait_recv()
    for i in range(3):
        total = yown[i]
        for d in range(1, 8):
            total = total + yrecv[d, i * 32 : (i + 1) * 32, :].astype(F32)
        zsend[i] = total.astype(BF16)
    zrecv[z] = zsend[zh]
    for d in range(1, 12):
        z_copy(d).start()

    cold_arrived(1, 0)
    cold_arrived(2, 0)
    for q in (1, 2):
        raw_copy(q, 1).wait_recv()
        place(q, 1)

    for d in range(1, 12):
        copy(zsend.at[zh], zrecv.at[(z + 12 - d) % 12], z_ss.at[d], z_rs.at[d], z_peer(d)).wait_recv()
    total = zrecv[0].astype(F32)
    for i in range(1, 12):
        total = total + zrecv[i].astype(F32)
    grecv[y] = total
    for d in range(1, 8):
        g_copy(d).start()

    cold_arrived(1, 1)
    cold_arrived(2, 1)
    adagrad(csum, ctab, cwas, cnow)
    cold_out.start()
    cold_accum_out.start()

    for d in range(1, 8):
        copy(grecv.at[y], grecv.at[(y + 8 - d) % 8], g_ss.at[d], g_rs.at[d], y_peer(d)).wait_recv()
    for i in range(8):
        hsum[i * 32 : (i + 1) * 32, :] = grecv[i]
    adagrad(hsum, htab, hwas, hnow)
    hot_out.start()
    hot_accum_out.start()

    for q in (1, 2):
        raw_copy(q, 1).wait_send()
        packed_copy(q).wait_send()
    ids_copy.wait_send()
    for i in range(HOT_FIELDS // 2):
        pair_copy(i).wait_send()

    def cold_sent(k, carry):
        for q in range(3):
            for h in range(2):
                cold_copy(q, h, k).wait_send()
        return carry

    lax.fori_loop(1, PLANE, cold_sent, 0)
    for d in range(1, 4):
        x_copy(d).wait_send()
    for d in range(1, 8):
        y_copy(d).wait_send()
        g_copy(d).wait_send()
    for d in range(1, 12):
        z_copy(d).wait_send()
    for out in (cold_out, cold_accum_out, hot_out, hot_accum_out):
        out.wait()


def hand_on_kernel(hot, hot_accum, cold, cold_accum, hot_out, hot_accum_out, cold_out, cold_accum_out, *held):
    sems = held[-1]
    rows = cold.shape[0] // PARTS
    ways = [(cold.at[pl.ds(i * rows, rows)], cold_out.at[pl.ds(i * rows, rows)]) for i in range(PARTS)]
    ways += [(hot, hot_out), (cold_accum, cold_accum_out), (hot_accum, hot_accum_out)]
    reads = [pltpu.make_async_copy(ways[i][0], held[i], sems.at[0, i]) for i in range(len(ways))]
    writes = [pltpu.make_async_copy(held[i], ways[i][1], sems.at[1, i]) for i in range(len(ways))]
    for read in reads:
        read.start()
    for read, write in zip(reads, writes):
        read.wait()
        write.start()
    for write in writes:
        write.wait()


def hand_on(*arrays):
    hbm = pl.BlockSpec(memory_space=pl.ANY)
    hot, hot_accum, cold, cold_accum = arrays
    held = [(cold.shape[0] // PARTS, E)] * PARTS + [hot.shape, cold_accum.shape, hot_accum.shape]
    return pl.pallas_call(
        hand_on_kernel,
        in_specs=[hbm] * 4,
        out_specs=[hbm] * 4,
        out_shape=[jax.ShapeDtypeStruct(each.shape, each.dtype) for each in arrays],
        scratch_shapes=[pltpu.VMEM(shape, F32) for shape in held] + [pltpu.SemaphoreType.DMA((2, len(held)))],
        compiler_params=pltpu.CompilerParams(vmem_limit_bytes=56 << 20),
        name="hand_on",
    )(*arrays)


def step(features, w_in, upstream, cold_table, hot_table, hot_ids, cold_rows, owners, cold_accum, hot_accum):
    hbm = pl.BlockSpec(memory_space=pl.ANY)
    dma = pltpu.SemaphoreType.DMA
    pairs = lambda *n: [dma(n), dma(n)]
    return pl.pallas_call(
        step_kernel,
        in_specs=[hbm] * 10,
        out_specs=[hbm] * 4,
        out_shape=[
            jax.ShapeDtypeStruct(each.shape, F32) for each in (hot_table, hot_accum, cold_table, cold_accum)
        ],
        scratch_shapes=[
            pltpu.VMEM(features.shape, BF16),
            pltpu.VMEM(w_in.shape, BF16),
            pltpu.VMEM(upstream.shape, BF16),
            pltpu.VMEM(hot_ids.shape, I32),
            pltpu.VMEM(cold_rows.shape, I32),
            pltpu.VMEM(owners.shape, I32),
            pltpu.VMEM(cold_accum.shape, F32),
            pltpu.VMEM(hot_accum.shape, F32),
            pltpu.VMEM(upstream.shape, F32),
            pltpu.VMEM(upstream.shape, BF16),
            pltpu.VMEM((2, HALF, LOOKUPS), BF16),
            pltpu.VMEM((HOT_FIELDS, SAMPLES, E), BF16),
            pltpu.VMEM((HOT_FIELDS, SAMPLES, E), BF16),
            pltpu.VMEM((HOT_FIELDS, SAMPLES), I32),
            pltpu.VMEM((2, HOT_FIELDS * SAMPLES, 2 * E), BF16),
            pltpu.VMEM((2, 768, 2 * E), F32),
            pltpu.VMEM((4, 768, E), BF16),
            pltpu.VMEM((4, 768, E), BF16),
            pltpu.VMEM((8, 96, E), BF16),
            pltpu.VMEM((3, 32, E), F32),
            pltpu.VMEM((8, 96, E), BF16),
            pltpu.VMEM((3, 32, E), BF16),
            pltpu.VMEM((12, 32, E), BF16),
            pltpu.VMEM((8, 32, E), F32),
            pltpu.VMEM((3, LOOKUPS, E), BF16),
            pltpu.VMEM((3, 1, LOOKUPS), I32),
            pltpu.VMEM((LOOKUPS, E), F32),
            pltpu.VMEM((3, LOOKUPS, E), BF16),
            pltpu.VMEM((3, 2, PLANE, SLOTS, E), BF16),
            pltpu.VMEM((3, 2, PLANE, DEPTH, E), BF16),
            pltpu.VMEM((OWNED, E), F32),
            pltpu.VMEM((256, E), F32),
            pltpu.VMEM((OWNED, E), F32),
            pltpu.VMEM((256, E), F32),
            pltpu.VMEM((OWNED, E), F32),
            pltpu.VMEM((256, E), F32),
            pltpu.VMEM((OWNED // E, E), F32),
            pltpu.VMEM((2, E), F32),
            dma((STEPS + 13,)),
        ]
        + pairs(3, 2) + pairs(3) + pairs(3, 2, PLANE) + pairs(5) + pairs(4) + pairs(8) + pairs(12) + pairs(8),
        compiler_params=pltpu.CompilerParams(
            collective_id=0, has_side_effects=True, vmem_limit_bytes=56 << 20
        ),
        name="step",
    )(features, w_in, upstream, cold_table, hot_table, hot_ids, cold_rows, owners, cold_accum, hot_accum)


def shards(
    features,
    w_in,
    upstream,
    hot_ids,
    cold_rows,
    cold_owner,
    hot_table,
    hot_accum,
    cold_table,
    cold_accum,
):
    results = step(
        features,
        w_in,
        upstream,
        cold_table,
        hot_table,
        hot_ids.T,
        cold_rows.reshape(1, -1),
        cold_owner.reshape(1, -1),
        cold_accum.reshape(-1, E),
        hot_accum.reshape(-1, E),
    )
    hot_new, hot_accum_new, cold_new, cold_accum_new = hand_on(*results)
    return (hot_new, hot_accum_new.reshape(-1), cold_new, cold_accum_new.reshape(-1))


def solution(mesh):
    placed = (
        P(("grp", "shard"), None),
        P(),
        P(("grp", "shard"), None),
        P(("grp", "shard"), None),
        P(("grp", "shard")),
        P(("grp", "shard"), None),
        P("shard", None),
        P("shard"),
        P(("grp", "shard"), None),
        P(("grp", "shard")),
    )
    return jax.shard_map(
        shards,
        mesh=mesh,
        in_specs=placed,
        out_specs=(P("shard", None), P("shard"), P(("grp", "shard"), None), P(("grp", "shard"))),
        check_vma=False,
    )
```

```python
import jax
import jax.numpy as jnp
from jax import lax
from jax.experimental import pallas as pl
from jax.experimental.pallas import tpu as pltpu
from jax.sharding import PartitionSpec as P

MESH = pl.DeviceIdType.MESH
learn_rate = 0.5

E = 128
SAMPLES = 256
HOT_FIELDS, COLD_FIELDS = 8, 4
PLANE = 8
LOOKUPS = 1024
SLOTS = 96
USED = 85
HEAD = 88
DEPTH = 128
HALF = 512
OWNED = 2048
STEPS = 3
BLOCK = 512
PARTS = 4
BF16, F32, I32 = jnp.bfloat16, jnp.float32, jnp.int32


def iota(shape, axis):
    return lax.broadcasted_iota(I32, shape, axis)


def nt_dot(a, b):
    return lax.dot_general(a, b, (((1,), (1,)), ((), ())), preferred_element_type=F32)


def dot(a, b):
    return jnp.dot(a, b, preferred_element_type=F32)


def step_kernel(
    feat_hbm, w_hbm, up_hbm, ctab_hbm, htab_hbm, hid_hbm, row_hbm, own_hbm, cacc_hbm, hacc_hbm,
    hot_hbm, hot_accum_hbm, cold_hbm, cold_accum_hbm,
    feat, w, up, hid_ref, row_ref, own_ref, cacc_ref, hacc_ref, pre, delta, order, hotg, hotg2, hid2, wide, hacc, xsend, xrecv, ysend, yown, yrecv, zsend, zrecv, grecv,
    raw, packed, loose, parts, csend, crecv, csum, hsum, ctab, htab, cwas, hwas, cnow, hnow,
    l_s, r_ss, r_rs, p_ss, p_rs, c_ss, c_rs, h_ss, h_rs, x_ss, x_rs, y_ss, y_rs, z_ss, z_rs, g_ss, g_rs,
):
    g, s = lax.axis_index("grp"), lax.axis_index("shard")
    zl, y = g // 8, g % 8
    zh, x, c = s // 8, (s // 2) % 4, s % 2
    z = zh * 4 + zl

    def at(zh, x, c):
        return (zh * 4 + x) * 2 + c

    def plane_peer(k):
        return (g, at(zh, (x + k // 2) % 4, (c + k % 2) % 2))

    def y_peer(d):
        return (zl * 8 + (y + d) % 8, s)

    def z_peer(d):
        to = (z + d) % 12
        return ((to % 4) * 8 + y, at(to // 4, x, c))

    def copy(src, dst, ss, rs, peer):
        return pltpu.make_async_remote_copy(
            src_ref=src, dst_ref=dst, send_sem=ss, recv_sem=rs, device_id=peer, device_id_type=MESH
        )

    def raw_copy(q, h):
        rows = pl.ds(h * HALF, HALF)
        return copy(raw.at[0, rows], raw.at[q, rows], r_ss.at[q, h], r_rs.at[q, h], (g, at((zh + q) % 3, x, c)))

    def packed_copy(q):
        return copy(packed.at[0], packed.at[q], p_ss.at[q], p_rs.at[q], (g, at((zh + q) % 3, x, c)))

    def cold_copy(q, h, k):
        return copy(
            csend.at[q, h, k], crecv.at[q, h, k, pl.ds(0, SLOTS)], c_ss.at[q, h, k], c_rs.at[q, h, k], plane_peer(k)
        )

    def pair_copy(i):
        return copy(
            hotg.at[pl.ds(2 * i, 2)], hotg2.at[pl.ds(2 * i, 2)], h_ss.at[i], h_rs.at[i], plane_peer(1)
        )

    ids_copy = copy(hid_ref, hid2, h_ss.at[4], h_rs.at[4], plane_peer(1))

    def x_copy(d):
        return copy(xsend.at[d], xrecv.at[d], x_ss.at[d], x_rs.at[d], plane_peer(2 * d))

    def y_copy(d):
        return copy(ysend.at[d], yrecv.at[d], y_ss.at[d], y_rs.at[d], y_peer(d))

    def z_copy(d):
        return copy(zsend.at[((z + d) % 12) // 4], zrecv.at[z], z_ss.at[d], z_rs.at[d], z_peer(d))

    def g_copy(d):
        return copy(grecv.at[y], grecv.at[y], g_ss.at[d], g_rs.at[d], y_peer(d))

    def load(src, dst, i):
        return pltpu.make_async_copy(src, dst, l_s.at[i])

    def w_copy(j):
        rows = pl.ds(pl.multiple_of(j * BLOCK, BLOCK), BLOCK)
        return load(w_hbm.at[rows], w.at[rows], j)

    own_copy, row_copy = load(own_hbm, own_ref, STEPS), load(row_hbm, row_ref, STEPS + 1)
    feat_copy, up_copy, hid_copy = (
        load(feat_hbm, feat, STEPS + 2), load(up_hbm, up, STEPS + 3), load(hid_hbm, hid_ref, STEPS + 4)
    )
    late_copies = (
        load(cacc_hbm, cacc_ref, STEPS + 5),
        load(hacc_hbm, hacc_ref, STEPS + 6),
        load(ctab_hbm, ctab, STEPS + 7),
        load(htab_hbm, htab, STEPS + 8),
    )
    cold_out, cold_accum_out = load(ctab, cold_hbm, STEPS + 9), load(cnow, cold_accum_hbm, STEPS + 10)
    hot_out, hot_accum_out = load(htab, hot_hbm, STEPS + 11), load(hnow, hot_accum_hbm, STEPS + 12)
    own_copy.start()
    row_copy.start()
    feat_copy.start()
    for j in range(STEPS):
        w_copy(j).start()
    up_copy.start()
    hid_copy.start()
    for late in late_copies:
        late.start()

    barrier = pltpu.get_barrier_semaphore()

    def greet(peer):
        pl.semaphore_signal(barrier, inc=1, device_id=peer, device_id_type=MESH)

    for d in (4, 8, 1, 2, 3, 5, 6, 7, 9, 10, 11):
        greet(z_peer(d))
    for k in range(1, PLANE):
        greet(plane_peer(k))
    for d in range(1, 8):
        greet(y_peer(d))

    crecv[:, :, :, SLOTS:, :] = jnp.zeros((3, 2, PLANE, DEPTH - SLOTS, E), BF16)
    csum[...] = jnp.zeros_like(csum)
    hacc[...] = jnp.zeros_like(hacc)
    pre[...] = jnp.zeros_like(pre)

    own_copy.wait()
    row_copy.wait()
    owner = own_ref[...]
    named = (owner == iota((32, LOOKUPS), 0)).astype(F32)
    before = (iota((256, 256), 0) < iota((256, 256), 1)).astype(BF16)
    carry = jnp.zeros((32, 1), F32)
    ranks = []
    for b in range(LOOKUPS // 256):
        block = named[:, b * 256 : (b + 1) * 256]
        count = dot(block.astype(BF16), before) + carry
        ranks.append(jnp.sum(block * count, axis=0, keepdims=True))
        carry = carry + jnp.sum(block, axis=1, keepdims=True)
    rank = jnp.concatenate(ranks, axis=1).astype(I32)
    first = jnp.sum(jnp.where(iota((32, LOOKUPS), 0) < owner, carry, 0.0), axis=0, keepdims=True).astype(I32)
    spot = first + rank
    spot = spot % 2 * HALF + spot // 2
    for h in range(2):
        order[h] = (spot - h * HALF == iota((HALF, LOOKUPS), 0)).astype(BF16)
    digit = iota((8, LOOKUPS), 0)
    row = row_ref[...]
    digits = jnp.where(digit == 0, owner, jnp.where(digit == 1, rank // 2, jnp.where(digit == 2, row // 128, row % 128)))
    digits = jnp.where(digit < 4, digits, 0).astype(F32).astype(BF16)

    feat_copy.wait()

    def preact_step(j, carry):
        w_copy(j).wait()
        columns = pl.ds(pl.multiple_of(j * BLOCK, BLOCK), BLOCK)
        pre[...] += dot(feat[:, columns], w[columns, :])
        return carry

    lax.fori_loop(0, STEPS, preact_step, 0)
    up_copy.wait()
    preact = pre[...]
    sigm = jax.nn.sigmoid(preact)
    delta[...] = (up[...].astype(F32) * sigm * (1.0 + preact * (1.0 - sigm))).astype(BF16)
    total = nt_dot(delta[...], w[HOT_FIELDS * E :, :])
    for f in range(COLD_FIELDS):
        loose[pl.ds(f, SAMPLES, stride=COLD_FIELDS), :] = total[:, f * E : (f + 1) * E]
    cold_rows = loose[...].astype(BF16)

    pl.semaphore_wait(barrier, 11 + 7 + 7)
    for h in range(2):
        raw[0, h * HALF : (h + 1) * HALF, :] = dot(order[h], cold_rows).astype(BF16)
    for q in (1, 2):
        raw_copy(q, 0).start()
    hid_copy.wait()
    ids_copy.start()

    def hot_step(i, carry):
        rows = pl.ds(pl.multiple_of(i * 2 * E, 2 * E), 2 * E)
        total = nt_dot(delta[...], w[rows, :])
        hotg[2 * i] = total[:, :E].astype(BF16)
        hotg[2 * i + 1] = total[:, E:].astype(BF16)
        pair_copy(i).start()
        return carry

    lax.fori_loop(0, HOT_FIELDS // 2, hot_step, 0)

    def hot_add(ids_ref, which, parity):
        ids = ids_ref[...]
        place = ids // 256
        away = ((place // 2) % 4 - x + 4) % 4
        inside = (place % 2 == c) & (away % 2 == parity)
        spot = jnp.where(inside, place // 8 * 256 + ids % 256, -1)
        for i in range(HOT_FIELDS // 2):
            chosen = jnp.concatenate(
                [(spot[2 * i + n : 2 * i + n + 1, :] == iota((768, SAMPLES), 0)).astype(BF16) for n in range(2)], axis=1
            )
            hacc[parity] += dot(chosen, wide[which, 2 * i * SAMPLES : (2 * i + 2) * SAMPLES, :])

    def widen(ids_ref, rows_ref, which):
        far = ((ids_ref[...] // 512) % 4 - x + 4) % 4 // 2
        far = far.astype(F32).T
        for f in range(HOT_FIELDS):
            keep = jnp.broadcast_to(far[:, f : f + 1], (SAMPLES, E)).astype(BF16)
            rows = rows_ref[f]
            second = rows * keep
            wide[which, f * SAMPLES : (f + 1) * SAMPLES, :E] = rows - second
            wide[which, f * SAMPLES : (f + 1) * SAMPLES, E:] = second

    widen(hid_ref, hotg, 0)
    hot_add(hid_ref, 0, 1)
    ids_copy.wait_recv()
    for i in range(HOT_FIELDS // 2):
        pair_copy(i).wait_recv()
    widen(hid2, hotg2, 1)
    hot_add(hid2, 1, 1)
    xsend[1] = hacc[1, :, :E].astype(BF16)
    x_copy(1).start()
    xsend[3] = hacc[1, :, E:].astype(BF16)
    x_copy(3).start()
    hot_add(hid_ref, 0, 0)
    hot_add(hid2, 1, 0)
    xsend[2] = hacc[0, :, E:].astype(BF16)
    x_copy(2).start()

    for h in range(2):
        sent = nt_dot(digits, order[h]).astype(I32)
        packed[0, :, h * HALF : (h + 1) * HALF] = ((sent[0:1] * 128 + sent[1:2]) * 16 + sent[2:3]) * 128 + sent[3:4]
    for q in (1, 2):
        packed_copy(q).start()

    which = iota((8, E), 0)
    column = iota((8, E), 1)
    pick = jnp.where(
        (which == 0) & (column == 0) | (which == 1) & (column == 1), 1.0, 0.0
    ).astype(BF16)

    def number(q):
        row = packed[q] % OWNED
        sort = iota((E, LOOKUPS), 0)
        parts[q] = jnp.where(sort == 0, row // 128, jnp.where(sort == 1, row % 128, 0)).astype(F32).T.astype(BF16)

    def place(q, h):
        rows = pl.ds(h * HALF, HALF)
        held = jnp.concatenate([raw[q, rows, :], parts[q, rows, :]], axis=1)
        slot = packed[q, :, rows] // OWNED - at(zh, 0, 0) * DEPTH
        for b in range(2):
            chosen = (slot - b * 4 * DEPTH == iota((4 * DEPTH, HALF), 0)).astype(BF16)
            filled = dot(chosen, held)
            numbers = nt_dot(pick, filled[:, E:].astype(BF16))
            for n in range(4):
                to = b * 4 + n
                half = filled[n * DEPTH : n * DEPTH + SLOTS, :E]
                tail = half[HEAD:] + numbers[:, n * DEPTH : (n + 1) * DEPTH]
                k = (to // 2 - x + 4) % 4 * 2 + (to % 2 - c + 2) % 2
                csend[q, h, k] = jnp.concatenate([half[:HEAD], tail], axis=0).astype(BF16)

        def send(k, carry):
            cold_copy(q, h, k).start()
            return carry

        lax.fori_loop(1, PLANE, send, 0)
        crecv[q, h, 0, :SLOTS, :] = csend[q, h, 0]

    def cold_add(q, h, ks):
        ids, rows = [], []
        for k in ks:
            tile = crecv[q, h, k, SLOTS - 16 : SLOTS, :].astype(F32)
            row = jnp.where(iota((1, E), 1) < USED, tile[8:9] * 128.0 + tile[9:10], -1.0)
            far = jnp.broadcast_to((row >= OWNED // 2).astype(F32), (8, DEPTH)).T
            keep = jnp.broadcast_to(far[:, :1], (DEPTH, E)).astype(BF16)
            arrived = crecv[q, h, k]
            second = arrived * keep
            rows.append(jnp.concatenate([arrived - second, second], axis=1))
            ids.append(row.astype(I32))
        ids, rows = jnp.concatenate(ids, axis=1), jnp.concatenate(rows, axis=0)
        ids = jnp.where(ids < 0, -1, ids % (OWNED // 2))
        for b in range(OWNED // 512):
            chosen = (ids - b * 256 == iota((256, ids.shape[1]), 0)).astype(BF16)
            total = dot(chosen, rows)
            csum[b * 256 : (b + 1) * 256, :] += total[:, :E]
            csum[OWNED // 2 + b * 256 : OWNED // 2 + (b + 1) * 256, :] += total[:, E:]

    def cold_arrived(q, h):
        for k in range(1, 4):
            cold_copy(q, h, k).wait_recv()
        cold_add(q, h, range(4))
        for k in range(4, 8):
            cold_copy(q, h, k).wait_recv()
        cold_add(q, h, range(4, 8))

    def spread(was, accum_ref):
        def block(b, carry):
            rows = pl.ds(pl.multiple_of(b * E, E), E)
            was[rows, :] = jnp.broadcast_to(accum_ref[pl.ds(b, 1), :], (E, E)).T
            return carry

        lax.fori_loop(0, accum_ref.shape[0], block, 0)

    def adagrad(sum_ref, table, was, now_ref, tiles):
        ones = jnp.ones((2 * E, E), BF16)
        corner = iota((tiles, E, E), 1) == iota((tiles, E, E), 2)

        def block(b, carry):
            rows = pl.ds(pl.multiple_of(b * tiles * E, tiles * E), tiles * E)
            grads = sum_ref[rows, :]
            square = grads * grads
            high = square.astype(BF16)
            low = (square - high.astype(F32)).astype(BF16)
            now = was[rows, :] + dot(jnp.concatenate([high, low], axis=1), ones) * (1.0 / E)
            table[rows, :] = table[rows, :] - learn_rate * grads / jnp.sqrt(now)
            now_ref[b] = jnp.sum(jnp.where(corner, now.reshape(tiles, E, E), 0.0), axis=1)
            return carry

        lax.fori_loop(0, now_ref.shape[0], block, 0)

    number(0)
    place(0, 0)
    place(0, 1)
    for q in (1, 2):
        raw_copy(q, 0).wait_send()
        raw_copy(q, 1).start()
    for late in late_copies:
        late.wait()
    spread(cwas, cacc_ref)
    spread(hwas, hacc_ref)

    for d in (1, 3, 2):
        x_copy(d).wait_recv()

    def over_x(i, carry):
        rows = pl.ds(pl.multiple_of(i * 256, 256), 256)
        total = hacc[0, rows, :E]
        for d in range(1, 4):
            total = total + xrecv[d, rows, :].astype(F32)
        hacc[0, rows, :E] = total
        return carry

    lax.fori_loop(0, 3, over_x, 0)

    def to_y(d, carry):
        for i in range(3):
            rows = pl.ds(pl.multiple_of(((y + d) % 8) * 32 + i * 256, 32), 32)
            ysend[d, i * 32 : (i + 1) * 32, :] = hacc[0, rows, :E].astype(BF16)
        y_copy(d).start()
        return carry

    lax.fori_loop(1, 8, to_y, 0)
    for i in range(3):
        yown[i] = hacc[0, pl.ds(pl.multiple_of(y * 32 + i * 256, 32), 32), :E]

    cold_arrived(0, 0)
    cold_arrived(0, 1)
    for q in (1, 2):
        packed_copy(q).wait_recv()
        number(q)
    for q in (1, 2):
        raw_copy(q, 0).wait_recv()
        place(q, 0)

    for d in range(1, 8):
        y_copy(d).wait_recv()
    for i in range(3):
        total = yown[i]
        for d in range(1, 8):
            total = total + yrecv[d, i * 32 : (i + 1) * 32, :].astype(F32)
        zsend[i] = total.astype(BF16)
    zrecv[z] = zsend[zh]
    for d in range(1, 12):
        z_copy(d).start()

    for q in (1, 2):
        raw_copy(q, 1).wait_recv()
        place(q, 1)

    for d in range(1, 12):
        copy(zsend.at[zh], zrecv.at[(z + 12 - d) % 12], z_ss.at[d], z_rs.at[d], z_peer(d)).wait_recv()
    total = zrecv[0].astype(F32)
    for i in range(1, 12):
        total = total + zrecv[i].astype(F32)
    grecv[y] = total
    for d in range(1, 8):
        g_copy(d).start()

    for h in range(2):
        for q in (1, 2):
            cold_arrived(q, h)
    adagrad(csum, ctab, cwas, cnow, 8)
    cold_out.start()
    cold_accum_out.start()

    for d in range(1, 8):
        copy(grecv.at[y], grecv.at[(y + 8 - d) % 8], g_ss.at[d], g_rs.at[d], y_peer(d)).wait_recv()
    for i in range(8):
        hsum[i * 32 : (i + 1) * 32, :] = grecv[i]
    adagrad(hsum, htab, hwas, hnow, 2)
    hot_out.start()
    hot_accum_out.start()

    for q in (1, 2):
        raw_copy(q, 1).wait_send()
        packed_copy(q).wait_send()
    ids_copy.wait_send()
    for i in range(HOT_FIELDS // 2):
        pair_copy(i).wait_send()

    def cold_sent(k, carry):
        for q in range(3):
            for h in range(2):
                cold_copy(q, h, k).wait_send()
        return carry

    lax.fori_loop(1, PLANE, cold_sent, 0)
    for d in range(1, 4):
        x_copy(d).wait_send()
    for d in range(1, 8):
        y_copy(d).wait_send()
        g_copy(d).wait_send()
    for d in range(1, 12):
        z_copy(d).wait_send()
    for out in (cold_out, cold_accum_out, hot_out, hot_accum_out):
        out.wait()


def hand_on_kernel(hot, hot_accum, cold, cold_accum, hot_out, hot_accum_out, cold_out, cold_accum_out, *held):
    sems = held[-1]
    rows = cold.shape[0] // PARTS
    ways = [(cold.at[pl.ds(i * rows, rows)], cold_out.at[pl.ds(i * rows, rows)]) for i in range(PARTS)]
    ways += [(hot, hot_out), (cold_accum, cold_accum_out), (hot_accum, hot_accum_out)]
    reads = [pltpu.make_async_copy(ways[i][0], held[i], sems.at[0, i]) for i in range(len(ways))]
    writes = [pltpu.make_async_copy(held[i], ways[i][1], sems.at[1, i]) for i in range(len(ways))]
    for read in reads:
        read.start()
    for read, write in zip(reads, writes):
        read.wait()
        write.start()
    for write in writes:
        write.wait()


def hand_on(*arrays):
    hbm = pl.BlockSpec(memory_space=pl.ANY)
    hot, hot_accum, cold, cold_accum = arrays
    held = [(cold.shape[0] // PARTS, E)] * PARTS + [hot.shape, cold_accum.shape, hot_accum.shape]
    return pl.pallas_call(
        hand_on_kernel,
        in_specs=[hbm] * 4,
        out_specs=[hbm] * 4,
        out_shape=[jax.ShapeDtypeStruct(each.shape, each.dtype) for each in arrays],
        scratch_shapes=[pltpu.VMEM(shape, F32) for shape in held] + [pltpu.SemaphoreType.DMA((2, len(held)))],
        compiler_params=pltpu.CompilerParams(vmem_limit_bytes=56 << 20),
        name="hand_on",
    )(*arrays)


def step(features, w_in, upstream, cold_table, hot_table, hot_ids, cold_rows, owners, cold_accum, hot_accum):
    hbm = pl.BlockSpec(memory_space=pl.ANY)
    dma = pltpu.SemaphoreType.DMA
    pairs = lambda *n: [dma(n), dma(n)]
    return pl.pallas_call(
        step_kernel,
        in_specs=[hbm] * 10,
        out_specs=[hbm] * 4,
        out_shape=[
            jax.ShapeDtypeStruct(shape, F32) for shape in (hot_table.shape, (1, 2, E), cold_table.shape, (2, 8, E))
        ],
        scratch_shapes=[
            pltpu.VMEM(features.shape, BF16),
            pltpu.VMEM(w_in.shape, BF16),
            pltpu.VMEM(upstream.shape, BF16),
            pltpu.VMEM(hot_ids.shape, I32),
            pltpu.VMEM(cold_rows.shape, I32),
            pltpu.VMEM(owners.shape, I32),
            pltpu.VMEM(cold_accum.shape, F32),
            pltpu.VMEM(hot_accum.shape, F32),
            pltpu.VMEM(upstream.shape, F32),
            pltpu.VMEM(upstream.shape, BF16),
            pltpu.VMEM((2, HALF, LOOKUPS), BF16),
            pltpu.VMEM((HOT_FIELDS, SAMPLES, E), BF16),
            pltpu.VMEM((HOT_FIELDS, SAMPLES, E), BF16),
            pltpu.VMEM((HOT_FIELDS, SAMPLES), I32),
            pltpu.VMEM((2, HOT_FIELDS * SAMPLES, 2 * E), BF16),
            pltpu.VMEM((2, 768, 2 * E), F32),
            pltpu.VMEM((4, 768, E), BF16),
            pltpu.VMEM((4, 768, E), BF16),
            pltpu.VMEM((8, 96, E), BF16),
            pltpu.VMEM((3, 32, E), F32),
            pltpu.VMEM((8, 96, E), BF16),
            pltpu.VMEM((3, 32, E), BF16),
            pltpu.VMEM((12, 32, E), BF16),
            pltpu.VMEM((8, 32, E), F32),
            pltpu.VMEM((3, LOOKUPS, E), BF16),
            pltpu.VMEM((3, 1, LOOKUPS), I32),
            pltpu.VMEM((LOOKUPS, E), F32),
            pltpu.VMEM((3, LOOKUPS, E), BF16),
            pltpu.VMEM((3, 2, PLANE, SLOTS, E), BF16),
            pltpu.VMEM((3, 2, PLANE, DEPTH, E), BF16),
            pltpu.VMEM((OWNED, E), F32),
            pltpu.VMEM((256, E), F32),
            pltpu.VMEM((OWNED, E), F32),
            pltpu.VMEM((256, E), F32),
            pltpu.VMEM((OWNED, E), F32),
            pltpu.VMEM((256, E), F32),
            pltpu.VMEM((2, 8, E), F32),
            pltpu.VMEM((1, 2, E), F32),
            dma((STEPS + 13,)),
        ]
        + pairs(3, 2) + pairs(3) + pairs(3, 2, PLANE) + pairs(5) + pairs(4) + pairs(8) + pairs(12) + pairs(8),
        compiler_params=pltpu.CompilerParams(
            collective_id=0, has_side_effects=True, vmem_limit_bytes=56 << 20
        ),
        name="step",
    )(features, w_in, upstream, cold_table, hot_table, hot_ids, cold_rows, owners, cold_accum, hot_accum)


def shards(
    features,
    w_in,
    upstream,
    hot_ids,
    cold_rows,
    cold_owner,
    hot_table,
    hot_accum,
    cold_table,
    cold_accum,
):
    results = step(
        features,
        w_in,
        upstream,
        cold_table,
        hot_table,
        hot_ids.T,
        cold_rows.reshape(1, -1),
        cold_owner.reshape(1, -1),
        cold_accum.reshape(-1, E),
        hot_accum.reshape(-1, E),
    )
    hot_new, hot_accum_new, cold_new, cold_accum_new = hand_on(*results)
    return (hot_new, hot_accum_new.reshape(-1), cold_new, cold_accum_new.reshape(-1))


def solution(mesh):
    placed = (
        P(("grp", "shard"), None),
        P(),
        P(("grp", "shard"), None),
        P(("grp", "shard"), None),
        P(("grp", "shard")),
        P(("grp", "shard"), None),
        P("shard", None),
        P("shard"),
        P(("grp", "shard"), None),
        P(("grp", "shard")),
    )
    return jax.shard_map(
        shards,
        mesh=mesh,
        in_specs=placed,
        out_specs=(P("shard", None), P("shard"), P(("grp", "shard"), None), P(("grp", "shard"))),
        check_vma=False,
    )
```

```python
import jax
import jax.numpy as jnp
from jax import lax
from jax.experimental import pallas as pl
from jax.experimental.pallas import tpu as pltpu
from jax.sharding import PartitionSpec as P

MESH = pl.DeviceIdType.MESH
learn_rate = 0.5

E = 128
SAMPLES = 256
HOT_FIELDS, COLD_FIELDS = 8, 4
PLANE = 8
LOOKUPS = 1024
SLOTS = 96
USED = 85
HEAD = 88
DEPTH = 128
HALF = 512
OWNED = 2048
STEPS = 6
BLOCK = 256
PARTS = 4
BF16, F32, I32 = jnp.bfloat16, jnp.float32, jnp.int32


def iota(shape, axis):
    return lax.broadcasted_iota(I32, shape, axis)


def nt_dot(a, b):
    return lax.dot_general(a, b, (((1,), (1,)), ((), ())), preferred_element_type=F32)


def dot(a, b):
    return jnp.dot(a, b, preferred_element_type=F32)


def step_kernel(
    feat_hbm, w_hbm, up_hbm, ctab_hbm, htab_hbm, hid_hbm, row_hbm, own_hbm, cacc_hbm, hacc_hbm,
    hot_hbm, hot_accum_hbm, cold_hbm, cold_accum_hbm,
    feat, w, up, hid_ref, row_ref, own_ref, cacc_ref, hacc_ref, pre, delta, order, hotg, hotg2, hid2, wide, hacc, xsend, xrecv, ysend, yown, yrecv, zsend, zrecv, grecv,
    raw, packed, loose, parts, csend, crecv, csum, hsum, ctab, htab, cwas, hwas, cnow, hnow,
    l_s, r_ss, r_rs, p_ss, p_rs, c_ss, c_rs, h_ss, h_rs, x_ss, x_rs, y_ss, y_rs, z_ss, z_rs, g_ss, g_rs,
):
    g, s = lax.axis_index("grp"), lax.axis_index("shard")
    zl, y = g // 8, g % 8
    zh, x, c = s // 8, (s // 2) % 4, s % 2
    z = zh * 4 + zl

    def at(zh, x, c):
        return (zh * 4 + x) * 2 + c

    def plane_peer(k):
        return (g, at(zh, (x + k // 2) % 4, (c + k % 2) % 2))

    def y_peer(d):
        return (zl * 8 + (y + d) % 8, s)

    def z_peer(d):
        to = (z + d) % 12
        return ((to % 4) * 8 + y, at(to // 4, x, c))

    def copy(src, dst, ss, rs, peer):
        return pltpu.make_async_remote_copy(
            src_ref=src, dst_ref=dst, send_sem=ss, recv_sem=rs, device_id=peer, device_id_type=MESH
        )

    def raw_copy(q, h):
        rows = pl.ds(h * HALF, HALF)
        return copy(raw.at[0, rows], raw.at[q, rows], r_ss.at[q, h], r_rs.at[q, h], (g, at((zh + q) % 3, x, c)))

    def packed_copy(q):
        return copy(packed.at[0], packed.at[q], p_ss.at[q], p_rs.at[q], (g, at((zh + q) % 3, x, c)))

    def cold_copy(q, h, k):
        return copy(
            csend.at[q, h, k], crecv.at[q, h, k, pl.ds(0, SLOTS)], c_ss.at[q, h, k], c_rs.at[q, h, k], plane_peer(k)
        )

    def pair_copy(i):
        return copy(
            hotg.at[pl.ds(2 * i, 2)], hotg2.at[pl.ds(2 * i, 2)], h_ss.at[i], h_rs.at[i], plane_peer(1)
        )

    ids_copy = copy(hid_ref, hid2, h_ss.at[4], h_rs.at[4], plane_peer(1))

    def x_copy(d):
        return copy(xsend.at[d], xrecv.at[d], x_ss.at[d], x_rs.at[d], plane_peer(2 * d))

    def y_copy(d):
        return copy(ysend.at[d], yrecv.at[d], y_ss.at[d], y_rs.at[d], y_peer(d))

    def z_copy(d):
        return copy(zsend.at[((z + d) % 12) // 4], zrecv.at[z], z_ss.at[d], z_rs.at[d], z_peer(d))

    def g_copy(d):
        return copy(grecv.at[y], grecv.at[y], g_ss.at[d], g_rs.at[d], y_peer(d))

    def load(src, dst, i):
        return pltpu.make_async_copy(src, dst, l_s.at[i])

    def w_copy(j):
        rows = pl.ds(pl.multiple_of(j * BLOCK, BLOCK), BLOCK)
        return load(w_hbm.at[rows], w.at[rows], j)

    own_copy, row_copy = load(own_hbm, own_ref, STEPS), load(row_hbm, row_ref, STEPS + 1)
    feat_copy, up_copy, hid_copy = (
        load(feat_hbm, feat, STEPS + 2), load(up_hbm, up, STEPS + 3), load(hid_hbm, hid_ref, STEPS + 4)
    )
    late_copies = (
        load(cacc_hbm, cacc_ref, STEPS + 5),
        load(hacc_hbm, hacc_ref, STEPS + 6),
        load(ctab_hbm, ctab, STEPS + 7),
        load(htab_hbm, htab, STEPS + 8),
    )
    cold_out, cold_accum_out = load(ctab, cold_hbm, STEPS + 9), load(cnow, cold_accum_hbm, STEPS + 10)
    hot_out, hot_accum_out = load(htab, hot_hbm, STEPS + 11), load(hnow, hot_accum_hbm, STEPS + 12)
    own_copy.start()
    row_copy.start()
    feat_copy.start()
    for j in range(STEPS):
        w_copy(j).start()
    up_copy.start()
    hid_copy.start()
    for late in late_copies:
        late.start()

    barrier = pltpu.get_barrier_semaphore()

    def greet(peer):
        pl.semaphore_signal(barrier, inc=1, device_id=peer, device_id_type=MESH)

    for d in (4, 8, 1, 2, 3, 5, 6, 7, 9, 10, 11):
        greet(z_peer(d))
    for k in range(1, PLANE):
        greet(plane_peer(k))
    for d in range(1, 8):
        greet(y_peer(d))

    crecv[:, :, :, SLOTS:, :] = jnp.zeros((3, 2, PLANE, DEPTH - SLOTS, E), BF16)
    csum[...] = jnp.zeros_like(csum)
    hacc[...] = jnp.zeros_like(hacc)
    pre[...] = jnp.zeros_like(pre)

    own_copy.wait()
    row_copy.wait()
    owner = own_ref[...]
    named = (owner == iota((32, LOOKUPS), 0)).astype(F32)
    before = (iota((256, 256), 0) < iota((256, 256), 1)).astype(BF16)
    carry = jnp.zeros((32, 1), F32)
    ranks = []
    for b in range(LOOKUPS // 256):
        block = named[:, b * 256 : (b + 1) * 256]
        count = dot(block.astype(BF16), before) + carry
        ranks.append(jnp.sum(block * count, axis=0, keepdims=True))
        carry = carry + jnp.sum(block, axis=1, keepdims=True)
    rank = jnp.concatenate(ranks, axis=1).astype(I32)
    first = jnp.sum(jnp.where(iota((32, LOOKUPS), 0) < owner, carry, 0.0), axis=0, keepdims=True).astype(I32)
    spot = first + rank
    spot = spot % 2 * HALF + spot // 2
    for h in range(2):
        order[h] = (spot - h * HALF == iota((HALF, LOOKUPS), 0)).astype(BF16)
    digit = iota((8, LOOKUPS), 0)
    row = row_ref[...]
    digits = jnp.where(digit == 0, owner, jnp.where(digit == 1, rank // 2, jnp.where(digit == 2, row // 128, row % 128)))
    digits = jnp.where(digit < 4, digits, 0).astype(F32).astype(BF16)

    feat_copy.wait()

    def preact_step(j, carry):
        w_copy(j).wait()
        columns = pl.ds(pl.multiple_of(j * BLOCK, BLOCK), BLOCK)
        pre[...] += dot(feat[:, columns], w[columns, :])
        return carry

    lax.fori_loop(0, STEPS, preact_step, 0)
    up_copy.wait()
    preact = pre[...]
    sigm = jax.nn.sigmoid(preact)
    delta[...] = (up[...].astype(F32) * sigm * (1.0 + preact * (1.0 - sigm))).astype(BF16)
    total = nt_dot(delta[...], w[HOT_FIELDS * E :, :])
    for f in range(COLD_FIELDS):
        loose[pl.ds(f, SAMPLES, stride=COLD_FIELDS), :] = total[:, f * E : (f + 1) * E]
    cold_rows = loose[...].astype(BF16)

    pl.semaphore_wait(barrier, 11 + 7 + 7)
    for h in range(2):
        raw[0, h * HALF : (h + 1) * HALF, :] = dot(order[h], cold_rows).astype(BF16)
    for q in (1, 2):
        raw_copy(q, 0).start()
    hid_copy.wait()
    ids_copy.start()

    def hot_step(i, carry):
        rows = pl.ds(pl.multiple_of(i * 2 * E, 2 * E), 2 * E)
        total = nt_dot(delta[...], w[rows, :])
        hotg[2 * i] = total[:, :E].astype(BF16)
        hotg[2 * i + 1] = total[:, E:].astype(BF16)
        pair_copy(i).start()
        return carry

    lax.fori_loop(0, HOT_FIELDS // 2, hot_step, 0)

    def hot_add(ids_ref, which, parity):
        ids = ids_ref[...]
        place = ids // 256
        away = ((place // 2) % 4 - x + 4) % 4
        inside = (place % 2 == c) & (away % 2 == parity)
        spot = jnp.where(inside, place // 8 * 256 + ids % 256, -1)
        for i in range(HOT_FIELDS // 2):
            chosen = jnp.concatenate(
                [(spot[2 * i + n : 2 * i + n + 1, :] == iota((768, SAMPLES), 0)).astype(BF16) for n in range(2)], axis=1
            )
            hacc[parity] += dot(chosen, wide[which, 2 * i * SAMPLES : (2 * i + 2) * SAMPLES, :])

    def widen(ids_ref, rows_ref, which):
        far = ((ids_ref[...] // 512) % 4 - x + 4) % 4 // 2
        far = far.astype(F32).T
        for f in range(HOT_FIELDS):
            keep = jnp.broadcast_to(far[:, f : f + 1], (SAMPLES, E)).astype(BF16)
            rows = rows_ref[f]
            second = rows * keep
            wide[which, f * SAMPLES : (f + 1) * SAMPLES, :E] = rows - second
            wide[which, f * SAMPLES : (f + 1) * SAMPLES, E:] = second

    widen(hid_ref, hotg, 0)
    hot_add(hid_ref, 0, 1)
    ids_copy.wait_recv()
    for i in range(HOT_FIELDS // 2):
        pair_copy(i).wait_recv()
    widen(hid2, hotg2, 1)
    hot_add(hid2, 1, 1)
    xsend[1] = hacc[1, :, :E].astype(BF16)
    x_copy(1).start()
    xsend[3] = hacc[1, :, E:].astype(BF16)
    x_copy(3).start()
    hot_add(hid_ref, 0, 0)
    hot_add(hid2, 1, 0)
    xsend[2] = hacc[0, :, E:].astype(BF16)
    x_copy(2).start()

    for h in range(2):
        sent = nt_dot(digits, order[h]).astype(I32)
        packed[0, :, h * HALF : (h + 1) * HALF] = ((sent[0:1] * 128 + sent[1:2]) * 16 + sent[2:3]) * 128 + sent[3:4]
    for q in (1, 2):
        packed_copy(q).start()

    which = iota((8, E), 0)
    column = iota((8, E), 1)
    pick = jnp.where(
        (which == 0) & (column == 0) | (which == 1) & (column == 1), 1.0, 0.0
    ).astype(BF16)

    def number(q):
        row = packed[q] % OWNED
        sort = iota((E, LOOKUPS), 0)
        parts[q] = jnp.where(sort == 0, row // 128, jnp.where(sort == 1, row % 128, 0)).astype(F32).T.astype(BF16)

    def place(q, h):
        rows = pl.ds(h * HALF, HALF)
        held = jnp.concatenate([raw[q, rows, :], parts[q, rows, :]], axis=1)
        slot = packed[q, :, rows] // OWNED - at(zh, 0, 0) * DEPTH
        for b in range(2):
            chosen = (slot - b * 4 * DEPTH == iota((4 * DEPTH, HALF), 0)).astype(BF16)
            filled = dot(chosen, held)
            numbers = nt_dot(pick, filled[:, E:].astype(BF16))
            for n in range(4):
                to = b * 4 + n
                half = filled[n * DEPTH : n * DEPTH + SLOTS, :E]
                tail = half[HEAD:] + numbers[:, n * DEPTH : (n + 1) * DEPTH]
                k = (to // 2 - x + 4) % 4 * 2 + (to % 2 - c + 2) % 2
                csend[q, h, k] = jnp.concatenate([half[:HEAD], tail], axis=0).astype(BF16)

        def send(k, carry):
            cold_copy(q, h, k).start()
            return carry

        lax.fori_loop(1, PLANE, send, 0)
        crecv[q, h, 0, :SLOTS, :] = csend[q, h, 0]

    def cold_add(q, h, ks):
        ids, rows = [], []
        for k in ks:
            tile = crecv[q, h, k, SLOTS - 16 : SLOTS, :].astype(F32)
            row = jnp.where(iota((1, E), 1) < USED, tile[8:9] * 128.0 + tile[9:10], -1.0)
            far = jnp.broadcast_to((row >= OWNED // 2).astype(F32), (8, DEPTH)).T
            keep = jnp.broadcast_to(far[:, :1], (DEPTH, E)).astype(BF16)
            arrived = crecv[q, h, k]
            second = arrived * keep
            rows.append(jnp.concatenate([arrived - second, second], axis=1))
            ids.append(row.astype(I32))
        ids, rows = jnp.concatenate(ids, axis=1), jnp.concatenate(rows, axis=0)
        ids = jnp.where(ids < 0, -1, ids % (OWNED // 2))
        for b in range(OWNED // 512):
            chosen = (ids - b * 256 == iota((256, ids.shape[1]), 0)).astype(BF16)
            total = dot(chosen, rows)
            csum[b * 256 : (b + 1) * 256, :] += total[:, :E]
            csum[OWNED // 2 + b * 256 : OWNED // 2 + (b + 1) * 256, :] += total[:, E:]

    def cold_arrived(q, h):
        for k in range(1, 4):
            cold_copy(q, h, k).wait_recv()
        cold_add(q, h, range(4))
        for k in range(4, 8):
            cold_copy(q, h, k).wait_recv()
        cold_add(q, h, range(4, 8))

    def spread(was, accum_ref):
        def block(b, carry):
            rows = pl.ds(pl.multiple_of(b * E, E), E)
            was[rows, :] = jnp.broadcast_to(accum_ref[pl.ds(b, 1), :], (E, E)).T
            return carry

        lax.fori_loop(0, accum_ref.shape[0], block, 0)

    def adagrad(sum_ref, table, was, now_ref, tiles):
        ones = jnp.ones((2 * E, E), BF16)
        corner = iota((tiles, E, E), 1) == iota((tiles, E, E), 2)

        def block(b, carry):
            rows = pl.ds(pl.multiple_of(b * tiles * E, tiles * E), tiles * E)
            grads = sum_ref[rows, :]
            square = grads * grads
            high = square.astype(BF16)
            low = (square - high.astype(F32)).astype(BF16)
            now = was[rows, :] + dot(jnp.concatenate([high, low], axis=1), ones) * (1.0 / E)
            table[rows, :] = table[rows, :] - learn_rate * grads / jnp.sqrt(now)
            now_ref[b] = jnp.sum(jnp.where(corner, now.reshape(tiles, E, E), 0.0), axis=1)
            return carry

        lax.fori_loop(0, now_ref.shape[0], block, 0)

    number(0)
    place(0, 0)
    place(0, 1)
    for q in (1, 2):
        raw_copy(q, 0).wait_send()
        raw_copy(q, 1).start()
    for late in late_copies:
        late.wait()
    spread(cwas, cacc_ref)
    spread(hwas, hacc_ref)

    for d in (1, 3, 2):
        x_copy(d).wait_recv()

    def over_x(i, carry):
        rows = pl.ds(pl.multiple_of(i * 256, 256), 256)
        total = hacc[0, rows, :E]
        for d in range(1, 4):
            total = total + xrecv[d, rows, :].astype(F32)
        hacc[0, rows, :E] = total
        return carry

    lax.fori_loop(0, 3, over_x, 0)

    def to_y(d, carry):
        for i in range(3):
            rows = pl.ds(pl.multiple_of(((y + d) % 8) * 32 + i * 256, 32), 32)
            ysend[d, i * 32 : (i + 1) * 32, :] = hacc[0, rows, :E].astype(BF16)
        y_copy(d).start()
        return carry

    lax.fori_loop(1, 8, to_y, 0)
    for i in range(3):
        yown[i] = hacc[0, pl.ds(pl.multiple_of(y * 32 + i * 256, 32), 32), :E]

    cold_arrived(0, 0)
    for q in (1, 2):
        packed_copy(q).wait_recv()
        number(q)
    for q in (1, 2):
        raw_copy(q, 0).wait_recv()
        place(q, 0)

    for d in range(1, 8):
        y_copy(d).wait_recv()
    for i in range(3):
        total = yown[i]
        for d in range(1, 8):
            total = total + yrecv[d, i * 32 : (i + 1) * 32, :].astype(F32)
        zsend[i] = total.astype(BF16)
    zrecv[z] = zsend[zh]
    for d in range(1, 12):
        z_copy(d).start()

    cold_arrived(0, 1)
    for q in (1, 2):
        raw_copy(q, 1).wait_recv()
        place(q, 1)

    for d in range(1, 12):
        copy(zsend.at[zh], zrecv.at[(z + 12 - d) % 12], z_ss.at[d], z_rs.at[d], z_peer(d)).wait_recv()
    total = zrecv[0].astype(F32)
    for i in range(1, 12):
        total = total + zrecv[i].astype(F32)
    grecv[y] = total
    for d in range(1, 8):
        g_copy(d).start()

    for h in range(2):
        for q in (1, 2):
            cold_arrived(q, h)
    adagrad(csum, ctab, cwas, cnow, 8)
    cold_out.start()
    cold_accum_out.start()

    for d in range(1, 8):
        copy(grecv.at[y], grecv.at[(y + 8 - d) % 8], g_ss.at[d], g_rs.at[d], y_peer(d)).wait_recv()
    for i in range(8):
        hsum[i * 32 : (i + 1) * 32, :] = grecv[i]
    adagrad(hsum, htab, hwas, hnow, 2)
    hot_out.start()
    hot_accum_out.start()

    for q in (1, 2):
        raw_copy(q, 1).wait_send()
        packed_copy(q).wait_send()
    ids_copy.wait_send()
    for i in range(HOT_FIELDS // 2):
        pair_copy(i).wait_send()

    def cold_sent(k, carry):
        for q in range(3):
            for h in range(2):
                cold_copy(q, h, k).wait_send()
        return carry

    lax.fori_loop(1, PLANE, cold_sent, 0)
    for d in range(1, 4):
        x_copy(d).wait_send()
    for d in range(1, 8):
        y_copy(d).wait_send()
        g_copy(d).wait_send()
    for d in range(1, 12):
        z_copy(d).wait_send()
    for out in (cold_out, cold_accum_out, hot_out, hot_accum_out):
        out.wait()


def hand_on_kernel(hot, hot_accum, cold, cold_accum, hot_out, hot_accum_out, cold_out, cold_accum_out, *held):
    sems = held[-1]
    rows = cold.shape[0] // PARTS
    ways = [(cold.at[pl.ds(i * rows, rows)], cold_out.at[pl.ds(i * rows, rows)]) for i in range(PARTS)]
    ways += [(hot, hot_out), (cold_accum, cold_accum_out), (hot_accum, hot_accum_out)]
    reads = [pltpu.make_async_copy(ways[i][0], held[i], sems.at[0, i]) for i in range(len(ways))]
    writes = [pltpu.make_async_copy(held[i], ways[i][1], sems.at[1, i]) for i in range(len(ways))]
    for read in reads:
        read.start()
    for read, write in zip(reads, writes):
        read.wait()
        write.start()
    for write in writes:
        write.wait()


def hand_on(*arrays):
    hbm = pl.BlockSpec(memory_space=pl.ANY)
    hot, hot_accum, cold, cold_accum = arrays
    held = [(cold.shape[0] // PARTS, E)] * PARTS + [hot.shape, cold_accum.shape, hot_accum.shape]
    return pl.pallas_call(
        hand_on_kernel,
        in_specs=[hbm] * 4,
        out_specs=[hbm] * 4,
        out_shape=[jax.ShapeDtypeStruct(each.shape, each.dtype) for each in arrays],
        scratch_shapes=[pltpu.VMEM(shape, F32) for shape in held] + [pltpu.SemaphoreType.DMA((2, len(held)))],
        compiler_params=pltpu.CompilerParams(vmem_limit_bytes=56 << 20),
        name="hand_on",
    )(*arrays)


def step(features, w_in, upstream, cold_table, hot_table, hot_ids, cold_rows, owners, cold_accum, hot_accum):
    hbm = pl.BlockSpec(memory_space=pl.ANY)
    dma = pltpu.SemaphoreType.DMA
    pairs = lambda *n: [dma(n), dma(n)]
    return pl.pallas_call(
        step_kernel,
        in_specs=[hbm] * 10,
        out_specs=[hbm] * 4,
        out_shape=[
            jax.ShapeDtypeStruct(shape, F32) for shape in (hot_table.shape, (1, 2, E), cold_table.shape, (2, 8, E))
        ],
        scratch_shapes=[
            pltpu.VMEM(features.shape, BF16),
            pltpu.VMEM(w_in.shape, BF16),
            pltpu.VMEM(upstream.shape, BF16),
            pltpu.VMEM(hot_ids.shape, I32),
            pltpu.VMEM(cold_rows.shape, I32),
            pltpu.VMEM(owners.shape, I32),
            pltpu.VMEM(cold_accum.shape, F32),
            pltpu.VMEM(hot_accum.shape, F32),
            pltpu.VMEM(upstream.shape, F32),
            pltpu.VMEM(upstream.shape, BF16),
            pltpu.VMEM((2, HALF, LOOKUPS), BF16),
            pltpu.VMEM((HOT_FIELDS, SAMPLES, E), BF16),
            pltpu.VMEM((HOT_FIELDS, SAMPLES, E), BF16),
            pltpu.VMEM((HOT_FIELDS, SAMPLES), I32),
            pltpu.VMEM((2, HOT_FIELDS * SAMPLES, 2 * E), BF16),
            pltpu.VMEM((2, 768, 2 * E), F32),
            pltpu.VMEM((4, 768, E), BF16),
            pltpu.VMEM((4, 768, E), BF16),
            pltpu.VMEM((8, 96, E), BF16),
            pltpu.VMEM((3, 32, E), F32),
            pltpu.VMEM((8, 96, E), BF16),
            pltpu.VMEM((3, 32, E), BF16),
            pltpu.VMEM((12, 32, E), BF16),
            pltpu.VMEM((8, 32, E), F32),
            pltpu.VMEM((3, LOOKUPS, E), BF16),
            pltpu.VMEM((3, 1, LOOKUPS), I32),
            pltpu.VMEM((LOOKUPS, E), F32),
            pltpu.VMEM((3, LOOKUPS, E), BF16),
            pltpu.VMEM((3, 2, PLANE, SLOTS, E), BF16),
            pltpu.VMEM((3, 2, PLANE, DEPTH, E), BF16),
            pltpu.VMEM((OWNED, E), F32),
            pltpu.VMEM((256, E), F32),
            pltpu.VMEM((OWNED, E), F32),
            pltpu.VMEM((256, E), F32),
            pltpu.VMEM((OWNED, E), F32),
            pltpu.VMEM((256, E), F32),
            pltpu.VMEM((2, 8, E), F32),
            pltpu.VMEM((1, 2, E), F32),
            dma((STEPS + 13,)),
        ]
        + pairs(3, 2) + pairs(3) + pairs(3, 2, PLANE) + pairs(5) + pairs(4) + pairs(8) + pairs(12) + pairs(8),
        compiler_params=pltpu.CompilerParams(
            collective_id=0, has_side_effects=True, vmem_limit_bytes=56 << 20
        ),
        name="step",
    )(features, w_in, upstream, cold_table, hot_table, hot_ids, cold_rows, owners, cold_accum, hot_accum)


def shards(
    features,
    w_in,
    upstream,
    hot_ids,
    cold_rows,
    cold_owner,
    hot_table,
    hot_accum,
    cold_table,
    cold_accum,
):
    results = step(
        features,
        w_in,
        upstream,
        cold_table,
        hot_table,
        hot_ids.T,
        cold_rows.reshape(1, -1),
        cold_owner.reshape(1, -1),
        cold_accum.reshape(-1, E),
        hot_accum.reshape(-1, E),
    )
    hot_new, hot_accum_new, cold_new, cold_accum_new = hand_on(*results)
    return (hot_new, hot_accum_new.reshape(-1), cold_new, cold_accum_new.reshape(-1))


def solution(mesh):
    placed = (
        P(("grp", "shard"), None),
        P(),
        P(("grp", "shard"), None),
        P(("grp", "shard"), None),
        P(("grp", "shard")),
        P(("grp", "shard"), None),
        P("shard", None),
        P("shard"),
        P(("grp", "shard"), None),
        P(("grp", "shard")),
    )
    return jax.shard_map(
        shards,
        mesh=mesh,
        in_specs=placed,
        out_specs=(P("shard", None), P("shard"), P(("grp", "shard"), None), P(("grp", "shard"))),
        check_vma=False,
    )
```
